128 devices in a mesh: ctx: 32 (over x, z, core), head: 4 (over y).
Axes of the slice: x: 4, y: 4, z: 4, core: 2. Of those that a mesh axis runs over, the one named last changes fastest.
Arguments:
- x_raw: bfloat16 [32768, 8192], P('ctx', 'head'), may hold values from -6 to 6
- z_gate: bfloat16 [32768, 8192], P('ctx', 'head'), may hold values from -6 to 6
- bc_raw: bfloat16 [32768, 256], P('ctx'), may hold values from -6 to 6
- conv_x: bfloat16 [4, 8192], P(None, 'head'), may hold values from -3 to 3
- conv_bc: bfloat16 [4, 256], replicated, may hold values from -3 to 3
- log_decay: float32 [32768, 128], P('ctx', 'head'), may hold values from -1.2 to 0
- step_size: float32 [32768, 128], P('ctx', 'head'), may hold values from 0.0005 to 0.005
- skip_coef: float32 [128], P('head'), may hold values from 0.4 to 6.1
- norm_gain: bfloat16 [8192], P('head'), may hold values from 0.5 to 1.5
- doc_starts: int32 [2], replicated, may hold values from 1 to 32767
Outputs:
- out: bfloat16 [32768, 8192], P('ctx', 'head')
The draws below stay inside these ranges and needn't reach their ends.
All inputs are finite; a program needn't handle non-finite values.
Results may differ from the reference program's by a relative error of at most 0.009.
Values may be sent and summed in bfloat16 or wider, within the bound.
A program may use at most 192 MiB of HBM per device.

```python
import math
import jax
import jax.numpy as jnp
from jax import lax

HEAD_TOTAL = 128
P_SIZE = 64
N = 128
BLOCK = 256
KCONV = 4
RESETS = 2
TOK_DEV = 1024
DI = 8192
WINDOW_TOKENS = 32768


def draw_log_decay(key, part):
    key = jax.random.fold_in(key, 17)
    random_subkeys = jax.random.split(key, 7)
    slow_share = 0.5
    slow_heads = jax.random.bernoulli(random_subkeys[0], slow_share, (HEAD_TOTAL,))
    fast_rate = 3.0 / jax.random.uniform(random_subkeys[1], (HEAD_TOTAL,), minval=30.0, maxval=50.0)
    slow_rate = math.log(10.0) / WINDOW_TOKENS * jax.random.uniform(random_subkeys[2], (HEAD_TOTAL,), minval=0.05, maxval=0.3)
    baseline_rate = jnp.where(slow_heads, slow_rate, fast_rate)
    block_multiplier = jnp.exp(jax.random.uniform(random_subkeys[3], (WINDOW_TOKENS // TOK_DEV, HEAD_TOTAL), minval=-0.9, maxval=0.9))
    block_multiplier = jnp.repeat(block_multiplier, TOK_DEV, axis=0)
    coarse_multiplier = jnp.exp(jax.random.uniform(random_subkeys[4], (WINDOW_TOKENS, HEAD_TOTAL), minval=-0.7, maxval=0.7))
    spike_positions = jax.random.randint(random_subkeys[5], (2,), 0, WINDOW_TOKENS)
    spike_rows = jnp.any(jnp.arange(WINDOW_TOKENS)[:, None] == spike_positions[None, :], axis=1)
    spike_loss = jnp.log(jax.random.uniform(random_subkeys[6], (WINDOW_TOKENS, HEAD_TOTAL), minval=0.5, maxval=0.8))
    return -baseline_rate[None, :] * block_multiplier * coarse_multiplier + jnp.where(spike_rows[:, None], spike_loss, 0.0)


def draw_skip_coef(key, part):
    key = jax.random.fold_in(key, 23)
    rising = 1.0 + 2.0 * jnp.arange(HEAD_TOTAL, dtype=jnp.float32) / HEAD_TOTAL
    spread = jnp.exp(jax.random.uniform(key, (HEAD_TOTAL,), minval=-0.7, maxval=0.7))
    return rising * spread


def steps_of(rng, extent, pieces, smallest, high):
    loudness = 1.0
    for axis_at, blocks in pieces:
        draws = jax.random.uniform(jax.random.fold_in(jax.random.fold_in(rng, 6), axis_at), (blocks,), jnp.float32, smallest / len(pieces), high / len(pieces))
        loudness = loudness * jnp.repeat(jnp.exp(draws), extent[axis_at] // blocks).reshape((-1,) + (1,) * (len(extent) - 1 - axis_at))
    return loudness


def scatter_about(own_key, dims, scale, most, cuts=(), held_as=jnp.bfloat16):
    values = jax.random.normal(own_key, dims, jnp.float32) * scale
    if len(cuts) > 0:
        values = steps_of(own_key, dims, cuts, -0.22, 0.18) * values
    return jnp.clip(values, min=-most, max=most).astype(held_as)


def setup_inputs(seed: int = 0) -> dict:
    key_of = jax.random.split(jax.random.key(seed), 11)
    return {
        "x_raw": scatter_about(key_of[0], (WINDOW_TOKENS, DI), 1.0, 6.0, ((0, 32), (1, 4))),
        "z_gate": scatter_about(key_of[1], (WINDOW_TOKENS, DI), 1.0, 6.0, ((0, 32), (1, 4))),
        "bc_raw": scatter_about(key_of[2], (WINDOW_TOKENS, 2 * N), 1.0, 6.0, ((0, 32),)),
        "conv_x": scatter_about(key_of[3], (KCONV, DI), KCONV ** -0.5, 3.0, ((1, 4),)),
        "conv_bc": scatter_about(key_of[4], (KCONV, 2 * N), KCONV ** -0.5, 3.0),
        "log_decay": draw_log_decay(jax.random.fold_in(key_of[10], 71), 0),
        "step_size": jnp.clip(jnp.exp(math.log(0.005) - 2.30258502 * jax.random.uniform(key_of[6], (WINDOW_TOKENS, HEAD_TOTAL), jnp.float32) ** steps_of(key_of[6], (WINDOW_TOKENS, HEAD_TOTAL), ((0, 32), (1, 4)), -0.2, 0.2)), 0.0005, 0.005),
        "skip_coef": draw_skip_coef(jax.random.fold_in(key_of[10], 71), 0),
        "norm_gain": jnp.clip(1.0 + 0.1 * jax.random.normal(key_of[8], (DI,), jnp.float32), 0.5, 1.5).astype(jnp.bfloat16),
        "doc_starts": jax.random.randint(key_of[9], (RESETS,), 1, WINDOW_TOKENS).astype(jnp.int32),
    }


def segment_count(doc_starts, positions):
    return lax.optimization_barrier(jnp.sum((doc_starts[None, :] <= positions[:, None]).astype(jnp.int32), axis=1))

def causal_conv(extended, tap_table, positions, seg_ext, row_count):
    margin = tap_table.shape[0] - 1
    tap_weights = tap_table.astype(jnp.float32)
    summed = jnp.zeros((row_count, extended.shape[1]), jnp.float32)
    for offset in range(tap_table.shape[0]):
        lower_row = margin - offset
        usable = (positions[lower_row:lower_row + row_count] >= 0) & (seg_ext[lower_row:lower_row + row_count] == seg_ext[margin:])
        summed = summed + tap_weights[offset] * extended[lower_row:lower_row + row_count].astype(jnp.float32) * usable[:, None].astype(jnp.float32)
    return jax.nn.silu(summed).astype(jnp.bfloat16)

def reference(x_raw, z_gate, bc_raw, conv_x, conv_bc, log_decay, step_size, skip_coef, norm_gain, doc_starts):
    margin = KCONV - 1
    block_count = WINDOW_TOKENS // BLOCK
    lower_tri = jnp.arange(BLOCK)[:, None] >= jnp.arange(BLOCK)[None, :]
    gain_wide = norm_gain.astype(jnp.float32)

    def block_step(carried, block_index):
        held_state, prev_x, prev_bc = carried
        first_token = block_index * BLOCK
        x_block = lax.dynamic_slice_in_dim(x_raw, first_token, BLOCK, 0)
        bc_block = lax.dynamic_slice_in_dim(bc_raw, first_token, BLOCK, 0)
        z_block = lax.dynamic_slice_in_dim(z_gate, first_token, BLOCK, 0)
        decay_block = lax.dynamic_slice_in_dim(log_decay, first_token, BLOCK, 0)
        step_block = lax.dynamic_slice_in_dim(step_size, first_token, BLOCK, 0)
        positions = first_token - margin + jnp.arange(BLOCK + margin, dtype=jnp.int32)
        seg_ext = segment_count(doc_starts, positions)
        seg_tok = seg_ext[margin:]
        seg_before = jnp.sum((doc_starts < first_token).astype(jnp.int32))
        conv_out = causal_conv(jnp.concatenate([prev_x, x_block], 0), conv_x, positions, seg_ext, BLOCK)
        bc_conv = causal_conv(jnp.concatenate([prev_bc, bc_block], 0), conv_bc, positions, seg_ext, BLOCK)
        b_state = bc_conv[:, :N]
        c_state = bc_conv[:, N:]
        log_cum = jnp.cumsum(decay_block, axis=0)
        x_heads = conv_out.reshape(BLOCK, HEAD_TOTAL, P_SIZE).astype(jnp.float32)
        u_in = (step_block[:, :, None] * x_heads).astype(jnp.bfloat16)
        scores = jnp.dot(c_state, b_state.T, preferred_element_type=jnp.float32)
        same_doc = lower_tri & (seg_tok[:, None] == seg_tok[None, :])
        log_gaps = log_cum.T[:, :, None] - log_cum.T[:, None, :]
        mix_weights = jnp.where(same_doc[None], scores[None] * jnp.exp(jnp.where(same_doc[None], log_gaps, 0.0)), 0.0).astype(jnp.bfloat16)
        intra_part = jnp.einsum('hij,jhp->ihp', mix_weights.astype(jnp.float32), u_in.astype(jnp.float32))
        opened = (seg_tok == seg_before).astype(jnp.float32)
        entry_decay = jnp.exp(log_cum) * opened[:, None]
        inter_part = entry_decay[:, :, None] * jnp.einsum('in,hpn->ihp', c_state.astype(jnp.float32), held_state, precision=lax.Precision.HIGHEST)
        summed = intra_part + inter_part + skip_coef[None, :, None] * x_heads
        gated_out = summed.reshape(BLOCK, HEAD_TOTAL * P_SIZE) * jax.nn.silu(z_block.astype(jnp.float32))
        mean_sq = lax.optimization_barrier(jnp.mean(gated_out * gated_out, axis=1, keepdims=True))
        result = (gated_out * lax.rsqrt(mean_sq + 1e-05) * gain_wide[None, :]).astype(jnp.bfloat16)
        closing = (seg_tok == seg_tok[-1]).astype(jnp.float32)
        to_end = step_block * jnp.exp(log_cum[-1][None, :] - log_cum) * closing[:, None]
        tail_input = (to_end[:, :, None] * x_heads).astype(jnp.bfloat16)
        fresh_state = jnp.einsum('shp,sn->hpn', tail_input.astype(jnp.float32), b_state.astype(jnp.float32))
        keep_factor = jnp.exp(log_cum[-1]) * (seg_tok[-1] == seg_before).astype(jnp.float32)
        held_state = keep_factor[:, None, None] * held_state + fresh_state
        return ((held_state, x_block[BLOCK - margin:], bc_block[BLOCK - margin:]), result)
    start_carry = (jnp.zeros((HEAD_TOTAL, P_SIZE, N), jnp.float32), jnp.zeros((margin, HEAD_TOTAL * P_SIZE), jnp.bfloat16), jnp.zeros((margin, 2 * N), jnp.bfloat16))
    final_carry, blocks_out = lax.scan(block_step, start_carry, jnp.arange(block_count, dtype=jnp.int32))
    return blocks_out.reshape(WINDOW_TOKENS, HEAD_TOTAL * P_SIZE)
```

```python
import functools

import jax
import jax.numpy as jnp
from jax import lax
from jax.experimental import pallas as pl
from jax.experimental.pallas import tpu as pltpu
from jax.sharding import PartitionSpec as P

MESH = pl.DeviceIdType.MESH
F32, BF16 = jnp.float32, jnp.bfloat16
L = 128
W = 256
HALO = 16
KROWS = 16
NN = (((1,), (0,)), ((), ()))
NT = (((1,), (1,)), ((), ()))


def dot(a, b, dims=NN, precision=None):
    return lax.dot_general(a, b, dims, precision=precision, preferred_element_type=F32)


def iota(shape, dim):
    return lax.broadcasted_iota(jnp.int32, shape, dim)


def split2(value):
    high = value.astype(BF16)
    return high, (value - high.astype(F32)).astype(BF16)


def layer_kernel(
    n, y_count, width_all,
    docs_ref, x_ref, z_ref, bc_ref, ld_ref, st_ref, cx_ref, cbc_ref, skip_ref,
    g_ref, rx_ref,
    xs, zs, bcs, lds, sts, xh, bch, es, smat, gmat, btm, cam, a_s, b_s, e_s, rows, rowsx,
    xcs, vs, hs, yl, sz, sp, rp, ap, ain, sq, sqx,
    load_sem, x_sem, z_sem, halo_send, halo_recv, send1, recv1, send2, recv2, send3, recv3,
):
    me = lax.axis_index("ctx")
    my = lax.axis_index("head")
    tokens, width = x_ref.shape
    heads = ld_ref.shape[1]
    chunks, tiles = tokens // L, width // W
    per_tile = 2 * W // 128
    pieces = per_tile * tiles
    ppo = pieces // n
    hd = width // heads
    first = me * tokens
    docs = [docs_ref[i] for i in range(docs_ref.shape[0])]
    tile0 = lax.rem(me * tiles // n, tiles)

    def tile_at(i):
        return lax.rem(tile0 + i, tiles)

    def cols(t):
        return pl.ds(pl.multiple_of(t * W, W), W)

    def x_copy(t):
        return pltpu.make_async_copy(x_ref.at[:, cols(t)], xs.at[:, cols(t)], x_sem.at[t])

    def z_copy(t):
        return pltpu.make_async_copy(z_ref.at[:, cols(t)], zs.at[:, cols(t)], z_sem.at[t])

    small = [
        pltpu.make_async_copy(ld_ref, lds, load_sem.at[0]),
        pltpu.make_async_copy(st_ref, sts, load_sem.at[1]),
        pltpu.make_async_copy(bc_ref, bcs, load_sem.at[2]),
    ]
    for copy in small:
        copy.start()
    for i in range(tiles):
        x_copy(tile_at(i)).start()
    for i in range(tiles):
        z_copy(tile_at(i)).start()

    barrier = pltpu.get_barrier_semaphore()

    def greet(i, carry):
        pl.semaphore_signal(
            barrier, inc=1, device_id={"ctx": lax.rem(me + i, n)}, device_id_type=MESH
        )
        return carry

    lax.fori_loop(1, n, greet, 0)
    for i in range(1, y_count):
        pl.semaphore_signal(
            barrier, inc=1, device_id={"head": lax.rem(my + i, y_count)}, device_id_type=MESH
        )

    es[...] = jnp.where(
        (iota((2 * heads, width), 1) // hd) == (iota((2 * heads, width), 0) & (heads - 1)), 1.0, 0.0
    ).astype(BF16)

    def crossed(low, high):
        hit = None
        for d in docs:
            one = (d > low) & (d <= high)
            hit = one if hit is None else hit | one
        return hit

    def put2(ref, at, value):
        high, low = split2(value)
        ref[at + (slice(None), slice(0, heads))] = high
        ref[at + (slice(None), slice(heads, 2 * heads))] = low

    small[0].wait()
    small[1].wait()
    tri = jnp.where(iota((L, L), 0) >= iota((L, L), 1), 1.0, 0.0)
    rows[...] = jnp.zeros_like(rows)
    base = jnp.zeros((1, heads), F32)
    centers, ends = [], []
    for q in range(chunks):
        at = slice(q * L, (q + 1) * L)
        lc = dot(tri, lds[at, :], precision=lax.Precision.HIGHEST)
        center, end = lc[L // 2 : L // 2 + 1, :], lc[L - 1 : L, :]
        centers.append(center)
        ends.append(end)
        put2(a_s, (q,), jnp.exp(lc - center))
        put2(b_s, (q,), jnp.exp(center - lc) * sts[at, :])
        put2(e_s, (q,), jnp.exp(base + lc))
        base = base + end
    for q in range(chunks):
        later = centers[q + 1] if q + 1 < chunks else jnp.zeros((1, heads), F32)
        k = jnp.exp(ends[q] - centers[q] + later)
        b = jnp.full((1, heads), first + q * L, jnp.int32)
        rows[q : q + 1, :] = jnp.where(crossed(b - 1, b + (L - 1)), 0.0, k)
        rows[chunks + q : chunks + q + 1, :] = k
    b = jnp.full((1, heads), first, jnp.int32)
    rows[2 * chunks : 2 * chunks + 1, :] = jnp.where(
        crossed(b - 1, b + (tokens - 1)), 0.0, jnp.exp(base)
    )
    rows[2 * chunks + 1 : 2 * chunks + 2, :] = skip_ref[...]
    r_high, r_low = split2(rows[...])
    rowsx[...] = dot(r_high, es[0:heads, :]) + dot(r_low, es[0:heads, :])

    t_at = iota((L, L), 0)
    s_at = iota((L, L), 1)
    lag_of = (s_at // HALO) + 1
    from_halo = (s_at - (lag_of - 1) * HALO == t_at + HALO - lag_of) & (s_at < 3 * HALO)
    for q in range(chunks):
        t_all = t_at + (first + q * L)
        for lag in range(1, 4):
            ok = (s_at == t_at - lag) & ~crossed(t_all - lag, t_all)
            smat[q, :, (lag - 1) * L : lag * L] = jnp.where(ok, 1.0, 0.0).astype(BF16)
        ok = from_halo & ~crossed(t_all - lag_of, t_all)
        smat[q, :, 3 * L : 4 * L] = jnp.where(ok, 1.0, 0.0).astype(BF16)

    pl.semaphore_wait(barrier, n - 1 + y_count - 1)

    def halo_copies():
        to = {"ctx": lax.rem(me + 1, n)}
        tail = pl.ds(tokens - HALO, HALO)
        return (
            pltpu.make_async_remote_copy(
                src_ref=x_ref.at[tail, :], dst_ref=xh, send_sem=halo_send.at[0],
                recv_sem=halo_recv.at[0], device_id=to, device_id_type=MESH,
            ),
            pltpu.make_async_remote_copy(
                src_ref=bc_ref.at[tail, :], dst_ref=bch, send_sem=halo_send.at[1],
                recv_sem=halo_recv.at[1], device_id=to, device_id_type=MESH,
            ),
        )

    @pl.when(me < n - 1)
    def _():
        for copy in halo_copies():
            copy.start()

    small[2].wait()

    @pl.when(me == 0)
    def _():
        xh[...] = jnp.zeros_like(xh)
        bch[...] = jnp.zeros_like(bch)

    @pl.when(me > 0)
    def _():
        for copy in halo_copies():
            copy.wait_recv()

    def conv_half(q, block, before, taps):
        taps16 = taps.astype(BF16)
        parts = [block * taps16[lag : lag + 1, :] for lag in range(1, 4)]
        parts += [before * taps16[lag : lag + 1, :] for lag in range(1, 4)]
        parts.append(jnp.zeros((L - 3 * HALO, W), BF16))
        moved = dot(smat[q], jnp.concatenate(parts, axis=0))
        return moved + block.astype(F32) * taps[0:1, :]

    def silu_of_half(half):
        return half + half * jnp.tanh(half)

    taps_bc = cbc_ref[...].astype(F32) * 0.5
    for q in range(chunks):
        block = bcs[q * L : (q + 1) * L, :]
        before = bch[...] if q == 0 else bcs[q * L - HALO : q * L, :]
        both = silu_of_half(conv_half(q, block, before, taps_bc))
        b_st, c_st = both[:, :128], both[:, 128:]
        t_all = t_at + (first + q * L)
        s_all = s_at + (first + q * L)
        b16, c16 = b_st.astype(BF16), c_st.astype(BF16)
        scores = dot(c16, b16, NT)
        ok = (s_at <= t_at) & ~crossed(s_all, t_all)
        gmat[q, :, 0:L] = jnp.where(ok, scores, 0.0).astype(BF16)
        begin = jnp.full((L, L), first + q * L, jnp.int32)
        gmat[q, :, L : 2 * L] = jnp.where(crossed(begin - 1, t_all), 0.0, c_st).astype(BF16)
        begin = jnp.full((L, L), first, jnp.int32)
        cam[q] = jnp.where(crossed(begin - 1, t_all), 0.0, c_st).astype(BF16)
        last = jnp.full((L, L), first + (q + 1) * L - 1, jnp.int32)
        btm[q] = jnp.transpose(jnp.where(crossed(t_all, last), 0.0, b_st)).astype(BF16)

    def piece_copy(p):
        owner = p // ppo
        return pltpu.make_async_remote_copy(
            src_ref=sp.at[p], dst_ref=rp.at[me, lax.rem(p, ppo)], send_sem=send1.at[p],
            recv_sem=recv1.at[me * ppo + lax.rem(p, ppo)],
            device_id={"ctx": owner}, device_id_type=MESH,
        )

    def pass_a(i, carry):
        t = tile_at(i)
        x_copy(t).wait()
        taps = cx_ref[:, cols(t)].astype(F32) * 0.5
        etile = es[:, cols(t)]
        state = jnp.zeros((128, W), F32)
        for q in range(chunks):
            at = slice(q * L, (q + 1) * L)
            block = xs[at, cols(t)]
            before = xh[:, cols(t)] if q == 0 else xs[q * L - HALO : q * L, cols(t)]
            xc = silu_of_half(conv_half(q, block, before, taps))
            xcs[at, cols(t)] = xc.astype(BF16)
            v = (xc * dot(b_s[q], etile)).astype(BF16)
            vs[at, cols(t)] = v
            hs[q, :, cols(t)] = state.astype(BF16)
            fresh = dot(btm[q], v)
            state = (
                rowsx[q : q + 1, cols(t)] * state
                + rowsx[chunks + q : chunks + q + 1, cols(t)] * fresh
            )
        keep = rowsx[2 * chunks : 2 * chunks + 1, cols(t)]
        keep_high = keep.astype(BF16).astype(F32)
        krow = iota((KROWS, W), 0)
        kblock = jnp.where(
            krow == 0, keep_high, jnp.where(krow == 1, keep - keep_high, 0.0)
        ).astype(BF16)
        for j in range(per_tile):
            p = t * per_tile + j
            lanes = slice((j // 2) * 128, (j // 2) * 128 + 128)
            sp[p, 0:64, :] = state[(j % 2) * 64 : (j % 2) * 64 + 64, lanes].astype(BF16)
            sp[p, 64 : 64 + KROWS, :] = kblock[:, lanes]

            @pl.when(p // ppo != me)
            def _():
                piece_copy(p).start()

            @pl.when(p // ppo == me)
            def _():
                rp[me, lax.rem(p, ppo)] = sp[p]

        return carry

    lax.fori_loop(0, tiles, pass_a, 0)

    def pass_b(i, carry):
        t = tile_at(i)
        z_copy(t).wait()
        etile = es[:, cols(t)]
        skip = rowsx[2 * chunks + 1 : 2 * chunks + 2, cols(t)]
        for q in range(chunks):
            at = slice(q * L, (q + 1) * L)
            mixed = dot(gmat[q], jnp.concatenate([vs[at, cols(t)], hs[q, :, cols(t)]], axis=0))
            own = mixed * dot(a_s[q], etile) + skip * xcs[at, cols(t)].astype(F32)
            yl[at, cols(t)] = own
            sz[at, cols(t)] = silu_of_half(zs[at, cols(t)].astype(F32) * 0.5)
        return carry

    split_b = 3
    lax.fori_loop(0, split_b, pass_b, 0)

    def piece_in(d, k):
        return pltpu.make_async_remote_copy(
            src_ref=sp.at[0], dst_ref=rp.at[d, k], send_sem=send1.at[0],
            recv_sem=recv1.at[d * ppo + k], device_id={"ctx": me}, device_id_type=MESH,
        )

    def enter_copy(d, k):
        return pltpu.make_async_remote_copy(
            src_ref=ap.at[d, k], dst_ref=ain.at[me * ppo + k], send_sem=send2.at[d * ppo + k],
            recv_sem=recv2.at[me * ppo + k], device_id={"ctx": d}, device_id_type=MESH,
        )

    def enter_in(p):
        return pltpu.make_async_remote_copy(
            src_ref=ap.at[0, 0], dst_ref=ain.at[p], send_sem=send2.at[0],
            recv_sem=recv2.at[p], device_id={"ctx": p // ppo}, device_id_type=MESH,
        )

    for k in range(ppo):
        def scan(d, state):
            @pl.when(d != me)
            def _():
                piece_in(d, k).wait_recv()

            ap[d, k] = state.astype(BF16)
            piece = rp[d, k].astype(F32)
            return (piece[64:65, :] + piece[65:66, :]) * state + piece[0:64, :]

        lax.fori_loop(0, n, scan, jnp.zeros((64, 128), F32))

        def spread(i, carry):
            enter_copy(lax.rem(me + i, n), k).start()
            return carry

        lax.fori_loop(1, n, spread, 0)
        ain[me * ppo + k] = ap[me, k]

    lax.fori_loop(split_b, tiles, pass_b, 0)

    sq[...] = jnp.zeros_like(sq)

    def pass_c(i, carry):
        t = tile_at(i)
        for j in range(per_tile):
            p = t * per_tile + j

            @pl.when(p // ppo != me)
            def _():
                enter_in(p).wait_recv()

        first_piece = t * per_tile
        entering = jnp.concatenate(
            [
                jnp.concatenate([ain[first_piece + 2 * j], ain[first_piece + 2 * j + 1]], axis=0)
                for j in range(per_tile // 2)
            ],
            axis=1,
        )
        etile = es[:, cols(t)]
        for q in range(chunks):
            at = slice(q * L, (q + 1) * L)
            inter = dot(cam[q], entering) * dot(e_s[q], etile)
            gated = (yl[at, cols(t)] + inter) * sz[at, cols(t)]
            g_ref[at, cols(t)] = gated.astype(BF16)
            squares = gated * gated
            sq[at, :] += squares[:, :128] + squares[:, 128:]
        return carry

    lax.fori_loop(0, tiles, pass_c, 0)

    total = jnp.zeros((8, L), F32)
    for q in range(chunks):
        pick = jnp.where(iota((8, 128), 0) == q, 1.0, 0.0).astype(BF16)
        high, low = split2(sq[q * L : (q + 1) * L, :])
        total = total + dot(pick, high, NT) + dot(pick, low, NT)
    sqx[0] = total

    def sq_copy(i):
        return pltpu.make_async_remote_copy(
            src_ref=sqx.at[0], dst_ref=sqx.at[i], send_sem=send3.at[i - 1],
            recv_sem=recv3.at[i - 1], device_id={"head": lax.rem(my + i, y_count)},
            device_id_type=MESH,
        )

    for i in range(1, y_count):
        sq_copy(i).start()
    for i in range(1, y_count):
        sq_copy(i).wait_recv()
    whole = sqx[0]
    for i in range(1, y_count):
        whole = whole + sqx[i]
    scale = lax.rsqrt(whole * (1.0 / width_all) + 1e-05)
    for q in range(chunks):
        rx_ref[q * L : (q + 1) * L, :] = jnp.transpose(
            jnp.broadcast_to(scale[q : q + 1, :], (128, L))
        )

    for i in range(1, y_count):
        sq_copy(i).wait_send()

    @pl.when(me < n - 1)
    def _():
        for copy in halo_copies():
            copy.wait_send()

    def drain1(p, carry):
        @pl.when(p // ppo != me)
        def _():
            piece_copy(p).wait_send()

        return carry

    lax.fori_loop(0, pieces, drain1, 0)
    for k in range(ppo):
        def drain2(i, carry):
            enter_copy(lax.rem(me + i, n), k).wait_send()
            return carry

        lax.fori_loop(1, n, drain2, 0)


def norm_kernel(g_ref, rx_ref, gain_ref, out_ref):
    rows, width = g_ref.shape
    scale = rx_ref[...]
    for j in range(width // 128):
        at = slice(j * 128, (j + 1) * 128)
        out_ref[:, at] = (
            g_ref[:, at].astype(F32) * scale * gain_ref[:, at].astype(F32)
        ).astype(BF16)


def per_device(
    n, y_count,
    x_raw, z_gate, bc_raw, conv_x, conv_bc, log_decay, step_size, skip_coef, norm_gain, doc_starts,
):
    tokens, width = x_raw.shape
    heads = log_decay.shape[1]
    chunks, tiles = tokens // L, width // W
    pieces = 4 * tiles
    ppo = pieces // n
    any_spec = pl.BlockSpec(memory_space=pl.ANY)
    vmem = pl.BlockSpec(memory_space=pltpu.VMEM)
    smem = pl.BlockSpec(memory_space=pltpu.SMEM)
    dma = pltpu.SemaphoreType.DMA
    gated, scale = pl.pallas_call(
        functools.partial(layer_kernel, n, y_count, float(width * y_count)),
        out_shape=(
            jax.ShapeDtypeStruct((tokens, width), BF16),
            jax.ShapeDtypeStruct((tokens, 128), F32),
        ),
        in_specs=[smem] + [any_spec] * 5 + [vmem] * 3,
        out_specs=(vmem, vmem),
        scratch_shapes=[
            pltpu.VMEM((tokens, width), BF16),
            pltpu.VMEM((tokens, width), BF16),
            pltpu.VMEM((tokens, 256), BF16),
            pltpu.VMEM((tokens, heads), F32),
            pltpu.VMEM((tokens, heads), F32),
            pltpu.VMEM((HALO, width), BF16),
            pltpu.VMEM((HALO, 256), BF16),
            pltpu.VMEM((2 * heads, width), BF16),
            pltpu.VMEM((chunks, L, 4 * L), BF16),
            pltpu.VMEM((chunks, L, 2 * L), BF16),
            pltpu.VMEM((chunks, 128, L), BF16),
            pltpu.VMEM((chunks, L, 128), BF16),
            pltpu.VMEM((chunks, L, 2 * heads), BF16),
            pltpu.VMEM((chunks, L, 2 * heads), BF16),
            pltpu.VMEM((chunks, L, 2 * heads), BF16),
            pltpu.VMEM((32, heads), F32),
            pltpu.VMEM((32, width), F32),
            pltpu.VMEM((tokens, width), BF16),
            pltpu.VMEM((tokens, width), BF16),
            pltpu.VMEM((chunks, 128, width), BF16),
            pltpu.VMEM((tokens, width), F32),
            pltpu.VMEM((tokens, width), F32),
            pltpu.VMEM((pieces, 64 + KROWS, 128), BF16),
            pltpu.VMEM((n, ppo, 64 + KROWS, 128), BF16),
            pltpu.VMEM((n, ppo, 64, 128), BF16),
            pltpu.VMEM((pieces, 64, 128), BF16),
            pltpu.VMEM((tokens, 128), F32),
            pltpu.VMEM((y_count, 8, 128), F32),
            dma((3,)), dma((tiles,)), dma((tiles,)), dma((2,)), dma((2,)),
            dma((pieces,)), dma((pieces,)), dma((pieces,)), dma((pieces,)),
            dma((y_count,)), dma((y_count,)),
        ],
        compiler_params=pltpu.CompilerParams(
            collective_id=0, has_side_effects=True, vmem_limit_bytes=60 * 1024 * 1024
        ),
        name="layer",
    )(
        doc_starts, x_raw, z_gate, bc_raw, log_decay, step_size, conv_x, conv_bc,
        skip_coef.reshape(1, heads),
    )
    block = 256
    return pl.pallas_call(
        norm_kernel,
        out_shape=jax.ShapeDtypeStruct((tokens, width), BF16),
        grid=(tokens // block,),
        in_specs=[
            pl.BlockSpec((block, width), lambda i: (i, 0)),
            pl.BlockSpec((block, 128), lambda i: (i, 0)),
            pl.BlockSpec((1, width), lambda i: (0, 0)),
        ],
        out_specs=pl.BlockSpec((block, width), lambda i: (i, 0)),
        name="norm",
    )(gated, scale, norm_gain.reshape(1, width))


def solution(mesh):
    in_specs = (
        P("ctx", "head"),
        P("ctx", "head"),
        P("ctx", None),
        P(None, "head"),
        P(),
        P("ctx", "head"),
        P("ctx", "head"),
        P("head"),
        P("head"),
        P(),
    )
    return jax.shard_map(
        functools.partial(per_device, mesh.shape["ctx"], mesh.shape["head"]),
        mesh=mesh, in_specs=in_specs, out_specs=P("ctx", "head"), check_vma=False,
    )
```

```python
import functools

import jax
import jax.numpy as jnp
from jax import lax
from jax.experimental import pallas as pl
from jax.experimental.pallas import tpu as pltpu
from jax.sharding import PartitionSpec as P

MESH = pl.DeviceIdType.MESH
F32, BF16 = jnp.float32, jnp.bfloat16
L = 128
W = 256
HALO = 16
KROWS = 16
NN = (((1,), (0,)), ((), ()))
NT = (((1,), (1,)), ((), ()))


def dot(a, b, dims=NN, precision=None):
    return lax.dot_general(a, b, dims, precision=precision, preferred_element_type=F32)


def iota(shape, dim):
    return lax.broadcasted_iota(jnp.int32, shape, dim)


def split2(value):
    high = value.astype(BF16)
    return high, (value - high.astype(F32)).astype(BF16)


def layer_kernel(
    n, y_count, width_all,
    docs_ref, x_ref, z_ref, bc_ref, ld_ref, st_ref, cx_hbm, cbc_hbm, skip_hbm,
    g_ref, rx_ref,
    xs, zs, bcs, lds, sts, cx_ref, cbc_ref, skip_ref, xh, bch, es, m1, m2, gbm, com, cam, a_s, b_s, e_s, rows, rowsx,
    xcs, hs, yl, sz, wide, wide2, sp, rp, ap, ain, sq, sqx,
    load_sem, x_sem, z_sem, halo_send, halo_recv, send1, recv1, send2, recv2, send3, recv3,
):
    me = lax.axis_index("ctx")
    my = lax.axis_index("head")
    tokens, width = x_ref.shape
    heads = ld_ref.shape[0]
    chunks, tiles = tokens // L, width // W
    per_tile = 2 * W // 128
    pieces = per_tile * tiles
    ppo = pieces // n
    hd = width // heads
    first = me * tokens
    docs = [docs_ref[i] for i in range(docs_ref.shape[0])]
    tile0 = lax.rem(me * tiles // n, tiles)

    def tile_at(i):
        return lax.rem(tile0 + i, tiles)

    def cols(t):
        return pl.ds(pl.multiple_of(t * W, W), W)

    def x_copy(t):
        return pltpu.make_async_copy(x_ref.at[:, cols(t)], xs.at[:, cols(t)], x_sem.at[t])

    def z_copy(t):
        return pltpu.make_async_copy(z_ref.at[:, cols(t)], zs.at[:, cols(t)], z_sem.at[t])

    small = [
        pltpu.make_async_copy(ld_ref, lds, load_sem.at[0]),
        pltpu.make_async_copy(st_ref, sts, load_sem.at[1]),
        pltpu.make_async_copy(bc_ref, bcs, load_sem.at[2]),
        pltpu.make_async_copy(cx_hbm, cx_ref, load_sem.at[3]),
        pltpu.make_async_copy(cbc_hbm, cbc_ref, load_sem.at[4]),
        pltpu.make_async_copy(skip_hbm, skip_ref, load_sem.at[5]),
    ]
    for copy in small:
        copy.start()
    for i in range(tiles):
        x_copy(tile_at(i)).start()
    for i in range(tiles):
        z_copy(tile_at(i)).start()

    barrier = pltpu.get_barrier_semaphore()

    def greet(i, carry):
        pl.semaphore_signal(
            barrier, inc=1, device_id={"ctx": lax.rem(me + i, n)}, device_id_type=MESH
        )
        return carry

    lax.fori_loop(1, n, greet, 0)
    for i in range(1, y_count):
        pl.semaphore_signal(
            barrier, inc=1, device_id={"head": lax.rem(my + i, y_count)}, device_id_type=MESH
        )

    es[...] = jnp.where(
        (iota((2 * heads, width), 1) // hd) == (iota((2 * heads, width), 0) & (heads - 1)), 1.0, 0.0
    ).astype(BF16)

    def crossed(low, high):
        hit = None
        for d in docs:
            one = (d > low) & (d <= high)
            hit = one if hit is None else hit | one
        return hit

    def put2(ref, q, value):
        high = value.astype(BF16).astype(F32)
        both = jnp.concatenate([high, value - high], axis=0)
        ref[q * L : (q + 1) * L, :] = jnp.transpose(both).astype(BF16)

    small[0].wait()
    small[1].wait()
    small[5].wait()
    tri = jnp.where(iota((L, L), 0) <= iota((L, L), 1), 1.0, 0.0)
    base = jnp.zeros((heads, 1), F32)
    centers, ends = [], []
    for q in range(chunks):
        at = slice(q * L, (q + 1) * L)
        lc = dot(lds[:, at], tri, precision=lax.Precision.HIGHEST)
        center, end = lc[:, L // 2 : L // 2 + 1], lc[:, L - 1 : L]
        centers.append(center)
        ends.append(end)
        put2(a_s, q, jnp.exp(lc - center))
        put2(b_s, q, jnp.exp(center - lc) * sts[:, at])
        put2(e_s, q, jnp.exp(base + lc))
        base = base + end
    lane = iota((heads, 128), 1)
    table = jnp.zeros((heads, 128), F32)
    for q in range(chunks):
        later = centers[q + 1] if q + 1 < chunks else jnp.zeros((heads, 1), F32)
        k = jnp.exp(ends[q] - centers[q] + later)
        b = jnp.full((heads, 1), first + q * L, jnp.int32)
        table = jnp.where(lane == q, jnp.where(crossed(b - 1, b + (L - 1)), 0.0, k), table)
        table = jnp.where(lane == chunks + q, k, table)
    b = jnp.full((heads, 1), first, jnp.int32)
    keep_all = jnp.where(crossed(b - 1, b + (tokens - 1)), 0.0, jnp.exp(base))
    table = jnp.where(lane == 2 * chunks, keep_all, table)
    rows[...] = jnp.transpose(table)[0:32, :]
    rows[2 * chunks + 1 : 2 * chunks + 2, :] = skip_ref[...]
    r_high, r_low = split2(rows[...])
    rowsx[...] = dot(r_high, es[0:heads, :]) + dot(r_low, es[0:heads, :])

    t_all = iota((HALO + tokens, 128), 0) + (first - HALO)
    m1[...] = jnp.where(crossed(t_all - 1, t_all), 0.0, 1.0)
    t_all = iota((tokens, 128), 0) + first
    m2[...] = jnp.where(crossed(t_all - 2, t_all), 0.0, 1.0)
    t_at = iota((L, L), 0)
    s_at = iota((L, L), 1)

    pl.semaphore_wait(barrier, n - 1 + y_count - 1)

    def halo_copies():
        to = {"ctx": lax.rem(me + 1, n)}
        tail = pl.ds(tokens - HALO, HALO)
        return (
            pltpu.make_async_remote_copy(
                src_ref=x_ref.at[tail, :], dst_ref=xh, send_sem=halo_send.at[0],
                recv_sem=halo_recv.at[0], device_id=to, device_id_type=MESH,
            ),
            pltpu.make_async_remote_copy(
                src_ref=bc_ref.at[tail, :], dst_ref=bch, send_sem=halo_send.at[1],
                recv_sem=halo_recv.at[1], device_id=to, device_id_type=MESH,
            ),
        )

    @pl.when(me < n - 1)
    def _():
        for copy in halo_copies():
            copy.start()

    small[2].wait()
    small[3].wait()
    small[4].wait()

    def conv_half(q, block, before, taps):
        ext = jnp.concatenate([before, block], axis=0).astype(F32)
        mask1 = m1[q * L : q * L + HALO + L, :]
        mask2 = m2[q * L : (q + 1) * L, :]
        ext1 = pltpu.roll(ext, 1, 0) * jnp.concatenate([mask1, mask1], axis=1)
        near = taps[0:1, :] * ext[HALO:] + taps[1:2, :] * ext1[HALO:]
        far = taps[2:3, :] * ext[8:] + taps[3:4, :] * ext1[8:]
        far = pltpu.roll(far, 2, 0)[8:]
        return near + far * jnp.concatenate([mask2, mask2], axis=1)

    def silu_of_half(half):
        return half + half * jnp.tanh(half)

    taps_bc = cbc_ref[...].astype(F32) * 0.5

    def shared(q, before):
        block = bcs[q * L : (q + 1) * L, :]
        both = silu_of_half(conv_half(q, block, before, taps_bc))
        b_st, c_st = both[:, :128], both[:, 128:]
        t_all = t_at + (first + q * L)
        s_all = s_at + (first + q * L)
        scores = dot(c_st.astype(BF16), b_st.astype(BF16), NT)
        ok = (s_at <= t_at) & ~crossed(s_all, t_all)
        gbm[q, 0:L, :] = jnp.where(ok, scores, 0.0).astype(BF16)
        last = jnp.full((L, L), first + (q + 1) * L - 1, jnp.int32)
        gbm[q, L : 2 * L, :] = jnp.transpose(jnp.where(crossed(t_all, last), 0.0, b_st)).astype(BF16)
        begin = jnp.full((L, L), first + q * L, jnp.int32)
        com[q] = jnp.where(crossed(begin - 1, t_all), 0.0, c_st).astype(BF16)
        begin = jnp.full((L, L), first, jnp.int32)
        cam[q * L : (q + 1) * L, :] = jnp.where(crossed(begin - 1, t_all), 0.0, c_st).astype(BF16)

    for q in range(1, chunks):
        shared(q, bcs[q * L - HALO : q * L, :])

    @pl.when(me == 0)
    def _():
        xh[...] = jnp.zeros_like(xh)
        bch[...] = jnp.zeros_like(bch)

    @pl.when(me > 0)
    def _():
        for copy in halo_copies():
            copy.wait_recv()

    shared(0, bch[...])

    def piece_copy(p):
        owner = p // ppo
        return pltpu.make_async_remote_copy(
            src_ref=sp.at[p], dst_ref=rp.at[me, lax.rem(p, ppo)], send_sem=send1.at[p],
            recv_sem=recv1.at[me * ppo + lax.rem(p, ppo)],
            device_id={"ctx": owner}, device_id_type=MESH,
        )

    def pass_a(i, carry):
        t = tile_at(i)
        x_copy(t).wait()
        taps = cx_ref[:, cols(t)].astype(F32) * 0.5
        etile = es[:, cols(t)]
        state = jnp.zeros((128, W), F32)
        wide[...] = dot(b_s[...], etile)
        for q in range(chunks):
            at = slice(q * L, (q + 1) * L)
            block = xs[at, cols(t)]
            before = xh[:, cols(t)] if q == 0 else xs[q * L - HALO : q * L, cols(t)]
            xc = silu_of_half(conv_half(q, block, before, taps))
            xcs[at, cols(t)] = xc.astype(BF16)
            v = (xc * wide[at, :]).astype(BF16)
            hs[q, :, cols(t)] = state.astype(BF16)
            both = dot(gbm[q], v)
            yl[at, cols(t)] = both[0:L, :]
            fresh = both[L:, :]
            state = (
                rowsx[q : q + 1, cols(t)] * state
                + rowsx[chunks + q : chunks + q + 1, cols(t)] * fresh
            )
        keep = rowsx[2 * chunks : 2 * chunks + 1, cols(t)]
        keep_high = keep.astype(BF16).astype(F32)
        krow = iota((KROWS, W), 0)
        kblock = jnp.where(
            krow == 0, keep_high, jnp.where(krow == 1, keep - keep_high, 0.0)
        ).astype(BF16)
        for j in range(per_tile):
            p = t * per_tile + j
            lanes = slice((j // 2) * 128, (j // 2) * 128 + 128)
            sp[p, 0:64, :] = state[(j % 2) * 64 : (j % 2) * 64 + 64, lanes].astype(BF16)
            sp[p, 64 : 64 + KROWS, :] = kblock[:, lanes]

            @pl.when(p // ppo != me)
            def _():
                piece_copy(p).start()

            @pl.when(p // ppo == me)
            def _():
                rp[me, lax.rem(p, ppo)] = sp[p]

        return carry

    lax.fori_loop(0, tiles, pass_a, 0)

    def pass_b(i, carry):
        t = tile_at(i)
        z_copy(t).wait()
        etile = es[:, cols(t)]
        skip = rowsx[2 * chunks + 1 : 2 * chunks + 2, cols(t)]
        wide[...] = dot(a_s[...], etile)
        for q in range(chunks):
            at = slice(q * L, (q + 1) * L)
            mixed = yl[at, cols(t)] + dot(com[q], hs[q, :, cols(t)])
            own = mixed * wide[at, :] + skip * xcs[at, cols(t)].astype(F32)
            yl[at, cols(t)] = own
            sz[at, cols(t)] = silu_of_half(zs[at, cols(t)].astype(F32) * 0.5)
        return carry

    split_b = 3
    lax.fori_loop(0, split_b, pass_b, 0)

    def piece_in(d, k):
        return pltpu.make_async_remote_copy(
            src_ref=sp.at[0], dst_ref=rp.at[d, k], send_sem=send1.at[0],
            recv_sem=recv1.at[d * ppo + k], device_id={"ctx": me}, device_id_type=MESH,
        )

    def enter_copy(d, k):
        return pltpu.make_async_remote_copy(
            src_ref=ap.at[d, k], dst_ref=ain.at[me * ppo + k], send_sem=send2.at[d * ppo + k],
            recv_sem=recv2.at[me * ppo + k], device_id={"ctx": d}, device_id_type=MESH,
        )

    def enter_in(p):
        return pltpu.make_async_remote_copy(
            src_ref=ap.at[0, 0], dst_ref=ain.at[p], send_sem=send2.at[0],
            recv_sem=recv2.at[p], device_id={"ctx": p // ppo}, device_id_type=MESH,
        )

    for k in range(ppo):
        def scan(d, state):
            @pl.when(d != me)
            def _():
                piece_in(d, k).wait_recv()

            ap[d, k] = state.astype(BF16)
            piece = rp[d, k].astype(F32)
            return (piece[64:65, :] + piece[65:66, :]) * state + piece[0:64, :]

        lax.fori_loop(0, n, scan, jnp.zeros((64, 128), F32))

        def spread(i, carry):
            enter_copy(lax.rem(me + i, n), k).start()
            return carry

        lax.fori_loop(1, n, spread, 0)
        ain[me * ppo + k] = ap[me, k]

    lax.fori_loop(split_b, tiles, pass_b, 0)

    sq[...] = jnp.zeros_like(sq)

    def pass_c(i, carry):
        t = tile_at(i)
        for j in range(per_tile):
            p = t * per_tile + j

            @pl.when(p // ppo != me)
            def _():
                enter_in(p).wait_recv()

        first_piece = t * per_tile
        entering = jnp.concatenate(
            [
                jnp.concatenate([ain[first_piece + 2 * j], ain[first_piece + 2 * j + 1]], axis=0)
                for j in range(per_tile // 2)
            ],
            axis=1,
        )
        etile = es[:, cols(t)]
        wide[...] = dot(e_s[...], etile)
        wide2[...] = dot(cam[...], entering)
        for q in range(chunks):
            at = slice(q * L, (q + 1) * L)
            gated = (yl[at, cols(t)] + wide2[at, :] * wide[at, :]) * sz[at, cols(t)]
            g_ref[at, cols(t)] = gated.astype(BF16)
            squares = gated * gated
            sq[at, :] += squares[:, :128] + squares[:, 128:]
        return carry

    lax.fori_loop(0, tiles, pass_c, 0)

    total = jnp.zeros((8, L), F32)
    for q in range(chunks):
        pick = jnp.where(iota((8, 128), 0) == q, 1.0, 0.0).astype(BF16)
        high, low = split2(sq[q * L : (q + 1) * L, :])
        total = total + dot(pick, high, NT) + dot(pick, low, NT)
    sqx[0] = total

    def sq_copy(i):
        return pltpu.make_async_remote_copy(
            src_ref=sqx.at[0], dst_ref=sqx.at[i], send_sem=send3.at[i - 1],
            recv_sem=recv3.at[i - 1], device_id={"head": lax.rem(my + i, y_count)},
            device_id_type=MESH,
        )

    for i in range(1, y_count):
        sq_copy(i).start()
    for i in range(1, y_count):
        sq_copy(i).wait_recv()
    whole = sqx[0]
    for i in range(1, y_count):
        whole = whole + sqx[i]
    scale = lax.rsqrt(whole * (1.0 / width_all) + 1e-05)
    for q in range(chunks):
        rx_ref[q * L : (q + 1) * L, :] = jnp.transpose(
            jnp.broadcast_to(scale[q : q + 1, :], (128, L))
        )

    for i in range(1, y_count):
        sq_copy(i).wait_send()

    @pl.when(me < n - 1)
    def _():
        for copy in halo_copies():
            copy.wait_send()

    def drain1(p, carry):
        @pl.when(p // ppo != me)
        def _():
            piece_copy(p).wait_send()

        return carry

    lax.fori_loop(0, pieces, drain1, 0)
    for k in range(ppo):
        def drain2(i, carry):
            enter_copy(lax.rem(me + i, n), k).wait_send()
            return carry

        lax.fori_loop(1, n, drain2, 0)


def norm_kernel(g_ref, rx_ref, gain_ref, out_ref, stage, sem):
    rows, width = g_ref.shape
    block = 128
    gain = gain_ref[...].reshape(1, width).astype(F32)

    def copy(i):
        at = pl.ds(i * block, block)
        return pltpu.make_async_copy(stage.at[at, :], out_ref.at[at, :], sem.at[i])

    for i in range(rows // block):
        at = slice(i * block, (i + 1) * block)
        scale = rx_ref[at, :]
        for j in range(width // 128):
            lanes = slice(j * 128, (j + 1) * 128)
            stage[at, lanes] = (g_ref[at, lanes].astype(F32) * scale * gain[:, lanes]).astype(BF16)
        copy(i).start()
    for i in range(rows // block):
        copy(i).wait()


def per_device(
    n, y_count,
    x_raw, z_gate, bc_raw, conv_x, conv_bc, log_decay, step_size, skip_coef, norm_gain, doc_starts,
):
    tokens, width = x_raw.shape
    heads = log_decay.shape[1]
    chunks, tiles = tokens // L, width // W
    pieces = 4 * tiles
    ppo = pieces // n
    any_spec = pl.BlockSpec(memory_space=pl.ANY)
    vmem = pl.BlockSpec(memory_space=pltpu.VMEM)
    smem = pl.BlockSpec(memory_space=pltpu.SMEM)
    dma = pltpu.SemaphoreType.DMA
    gated, scale = pl.pallas_call(
        functools.partial(layer_kernel, n, y_count, float(width * y_count)),
        out_shape=(
            pltpu.VMEM((tokens, width), BF16),
            pltpu.VMEM((tokens, 128), F32),
        ),
        in_specs=[smem] + [any_spec] * 8,
        out_specs=(vmem, vmem),
        scratch_shapes=[
            pltpu.VMEM((tokens, width), BF16),
            pltpu.VMEM((tokens, width), BF16),
            pltpu.VMEM((tokens, 256), BF16),
            pltpu.VMEM((heads, tokens), F32),
            pltpu.VMEM((heads, tokens), F32),
            pltpu.VMEM((4, width), BF16),
            pltpu.VMEM((4, 256), BF16),
            pltpu.VMEM((1, heads), F32),
            pltpu.VMEM((HALO, width), BF16),
            pltpu.VMEM((HALO, 256), BF16),
            pltpu.VMEM((2 * heads, width), BF16),
            pltpu.VMEM((HALO + tokens, 128), F32),
            pltpu.VMEM((tokens, 128), F32),
            pltpu.VMEM((chunks, 2 * L, L), BF16),
            pltpu.VMEM((chunks, L, 128), BF16),
            pltpu.VMEM((tokens, 128), BF16),
            pltpu.VMEM((tokens, 2 * heads), BF16),
            pltpu.VMEM((tokens, 2 * heads), BF16),
            pltpu.VMEM((tokens, 2 * heads), BF16),
            pltpu.VMEM((32, heads), F32),
            pltpu.VMEM((32, width), F32),
            pltpu.VMEM((tokens, width), BF16),
            pltpu.VMEM((chunks, 128, width), BF16),
            pltpu.VMEM((tokens, width), F32),
            pltpu.VMEM((tokens, width), F32),
            pltpu.VMEM((tokens, W), F32),
            pltpu.VMEM((tokens, W), F32),
            pltpu.VMEM((pieces, 64 + KROWS, 128), BF16),
            pltpu.VMEM((n, ppo, 64 + KROWS, 128), BF16),
            pltpu.VMEM((n, ppo, 64, 128), BF16),
            pltpu.VMEM((pieces, 64, 128), BF16),
            pltpu.VMEM((tokens, 128), F32),
            pltpu.VMEM((y_count, 8, 128), F32),
            dma((6,)), dma((tiles,)), dma((tiles,)), dma((2,)), dma((2,)),
            dma((pieces,)), dma((pieces,)), dma((pieces,)), dma((pieces,)),
            dma((y_count,)), dma((y_count,)),
        ],
        compiler_params=pltpu.CompilerParams(
            collective_id=0, has_side_effects=True, vmem_limit_bytes=59 * 1024 * 1024
        ),
        name="layer",
    )(
        doc_starts, x_raw, z_gate, bc_raw, log_decay.T, step_size.T, conv_x, conv_bc,
        skip_coef.reshape(1, heads),
    )
    return pl.pallas_call(
        norm_kernel,
        out_shape=jax.ShapeDtypeStruct((tokens, width), BF16),
        in_specs=[vmem] * 3,
        out_specs=any_spec,
        scratch_shapes=[pltpu.VMEM((tokens, width), BF16), dma((tokens // 128,))],
        compiler_params=pltpu.CompilerParams(vmem_limit_bytes=16 * 1024 * 1024),
        name="norm",
    )(gated, scale, norm_gain)


def solution(mesh):
    in_specs = (
        P("ctx", "head"),
        P("ctx", "head"),
        P("ctx", None),
        P(None, "head"),
        P(),
        P("ctx", "head"),
        P("ctx", "head"),
        P("head"),
        P("head"),
        P(),
    )
    return jax.shard_map(
        functools.partial(per_device, mesh.shape["ctx"], mesh.shape["head"]),
        mesh=mesh, in_specs=in_specs, out_specs=P("ctx", "head"), check_vma=False,
    )
```

```python
import functools

import jax
import jax.numpy as jnp
from jax import lax
from jax.experimental import pallas as pl
from jax.experimental.pallas import tpu as pltpu
from jax.sharding import PartitionSpec as P

MESH = pl.DeviceIdType.MESH
F32, BF16 = jnp.float32, jnp.bfloat16
L = 128
W = 256
HALO = 16
KROWS = 16
NN = (((1,), (0,)), ((), ()))
NT = (((1,), (1,)), ((), ()))


def dot(a, b, dims=NN, precision=None):
    return lax.dot_general(a, b, dims, precision=precision, preferred_element_type=F32)


def iota(shape, dim):
    return lax.broadcasted_iota(jnp.int32, shape, dim)


def split2(value):
    high = value.astype(BF16)
    return high, (value - high.astype(F32)).astype(BF16)


def layer_kernel(
    n, y_count, width_all,
    docs_ref, x_ref, z_ref, bc_ref, ld_ref, st_ref, cx_hbm, cbc_hbm, skip_hbm,
    g_ref, rx_ref,
    xs, zs, bcs, lds, sts, cx_ref, cbc_ref, skip_ref, xh, bch, es, m1, m2, gbm, com, cam, a_s, b_s, e_s, rows, rowsx,
    xcs, hs, yl, sz, wide, wide2, sp, ex, sc, rp, ap, ain, fw, ent, sq, sqx,
    load_sem, x_sem, z_sem, halo_send, halo_recv, ex_send, ex_recv, send1, recv1, send2, recv2,
    fw_send, fw_recv, send3, recv3,
):
    me = lax.axis_index("ctx")
    my = lax.axis_index("head")
    tokens, width = x_ref.shape
    heads = ld_ref.shape[0]
    chunks, tiles = tokens // L, width // W
    pairs = width // 128
    per_tile = W // 128
    chips = n // 2
    ppc = pairs // chips
    chip, core = me // 2, lax.rem(me, 2)
    peer = me + 1 - 2 * core
    own_rows = pl.ds(pl.multiple_of(core * 64, 64), 64)
    hd = width // heads
    first = me * tokens
    docs = [docs_ref[i] for i in range(docs_ref.shape[0])]
    tile0 = lax.rem(chip * tiles // chips, tiles)

    def tile_at(i):
        return lax.rem(tile0 + i, tiles)

    def cols(t):
        return pl.ds(pl.multiple_of(t * W, W), W)

    def x_copy(t):
        return pltpu.make_async_copy(x_ref.at[:, cols(t)], xs.at[:, cols(t)], x_sem.at[t])

    def z_copy(t):
        return pltpu.make_async_copy(z_ref.at[:, cols(t)], zs.at[:, cols(t)], z_sem.at[t])

    barrier = pltpu.get_barrier_semaphore()

    def greet(device):
        pl.semaphore_signal(barrier, inc=1, device_id=device, device_id_type=MESH)

    greet({"ctx": peer})
    greet({"ctx": lax.rem(me + n - 1 + 2 * core, n)})
    for i in range(1, chips):
        greet({"ctx": lax.rem(me + 2 * i, n)})
    for i in range(1, y_count):
        greet({"head": lax.rem(my + i, y_count)})

    small = [
        pltpu.make_async_copy(ld_ref, lds, load_sem.at[0]),
        pltpu.make_async_copy(st_ref, sts, load_sem.at[1]),
        pltpu.make_async_copy(bc_ref, bcs, load_sem.at[2]),
        pltpu.make_async_copy(cx_hbm, cx_ref, load_sem.at[3]),
        pltpu.make_async_copy(cbc_hbm, cbc_ref, load_sem.at[4]),
        pltpu.make_async_copy(skip_hbm, skip_ref, load_sem.at[5]),
    ]
    for copy in small:
        copy.start()
    for i in range(tiles):
        x_copy(tile_at(i)).start()
    for i in range(tiles):
        z_copy(tile_at(i)).start()

    es[...] = jnp.where(
        (iota((2 * heads, width), 1) // hd) == (iota((2 * heads, width), 0) & (heads - 1)), 1.0, 0.0
    ).astype(BF16)

    def crossed(low, high):
        hit = None
        for d in docs:
            one = (d > low) & (d <= high)
            hit = one if hit is None else hit | one
        return hit

    def put2(ref, value):
        high = value.astype(BF16).astype(F32)
        low = value - high
        for q in range(chunks):
            at = slice(q * heads, (q + 1) * heads)
            both = jnp.concatenate([high[at], low[at]], axis=0)
            ref[q * L : (q + 1) * L, :] = jnp.transpose(both).astype(BF16)

    small[0].wait()
    small[1].wait()
    small[5].wait()
    tri = jnp.where(iota((L, L), 0) <= iota((L, L), 1), 1.0, 0.0).astype(BF16)
    ld = jnp.concatenate([lds[:, q * L : (q + 1) * L] for q in range(chunks)], axis=0)
    st = jnp.concatenate([sts[:, q * L : (q + 1) * L] for q in range(chunks)], axis=0)
    high, mid = split2(ld)
    low = (ld - high.astype(F32) - mid.astype(F32)).astype(BF16)
    sums = dot(jnp.concatenate([high, mid, low], axis=0), tri)
    rows_all = chunks * heads
    lc = sums[0:rows_all] + (sums[rows_all : 2 * rows_all] + sums[2 * rows_all :])
    center, end = lc[:, L // 2 : L // 2 + 1], lc[:, L - 1 : L]
    bases = [jnp.zeros((heads, 1), F32)]
    for q in range(chunks):
        bases.append(bases[-1] + end[q * heads : (q + 1) * heads])
    base = bases[-1]
    put2(a_s, jnp.exp(lc - center))
    put2(b_s, jnp.exp(center - lc) * st)
    put2(e_s, jnp.exp(jnp.concatenate(bases[:-1], axis=0) + lc))
    centers = [center[q * heads : (q + 1) * heads] for q in range(chunks)]
    ends = [end[q * heads : (q + 1) * heads] for q in range(chunks)]

    pl.semaphore_wait(barrier, chips + 1 + y_count - 1)

    def halo_copies():
        to = {"ctx": lax.rem(me + 1, n)}
        tail = pl.ds(tokens - HALO, HALO)
        return (
            pltpu.make_async_remote_copy(
                src_ref=x_ref.at[tail, :], dst_ref=xh, send_sem=halo_send.at[0],
                recv_sem=halo_recv.at[0], device_id=to, device_id_type=MESH,
            ),
            pltpu.make_async_remote_copy(
                src_ref=bc_ref.at[tail, :], dst_ref=bch, send_sem=halo_send.at[1],
                recv_sem=halo_recv.at[1], device_id=to, device_id_type=MESH,
            ),
        )

    @pl.when(me < n - 1)
    def _():
        for copy in halo_copies():
            copy.start()

    lane = iota((heads, 128), 1)
    table = jnp.zeros((heads, 128), F32)
    for q in range(chunks):
        later = centers[q + 1] if q + 1 < chunks else jnp.zeros((heads, 1), F32)
        k = jnp.exp(ends[q] - centers[q] + later)
        b = jnp.full((heads, 1), first + q * L, jnp.int32)
        table = jnp.where(lane == q, jnp.where(crossed(b - 1, b + (L - 1)), 0.0, k), table)
        table = jnp.where(lane == chunks + q, k, table)
    b = jnp.full((heads, 1), first, jnp.int32)
    keep_all = jnp.where(crossed(b - 1, b + (tokens - 1)), 0.0, jnp.exp(base))
    table = jnp.where(lane == 2 * chunks, keep_all, table)
    rows[...] = jnp.transpose(table)[0:32, :]
    rows[2 * chunks + 1 : 2 * chunks + 2, :] = skip_ref[...]
    r_high, r_low = split2(rows[...])
    rowsx[...] = dot(r_high, es[0:heads, :]) + dot(r_low, es[0:heads, :])

    def expand_b(i, carry):
        at = pl.ds(pl.multiple_of(i * 512, 512), 512)
        xcs[:, at] = dot(b_s[...], es[:, at]).astype(BF16)
        return carry

    lax.fori_loop(0, width // 512, expand_b, 0)

    def any_of(conditions):
        hit = conditions[0]
        for one in conditions[1:]:
            hit = hit | one
        return hit

    row8 = iota((8, 128), 0)
    for r in range(0, HALO + tokens, 8):
        starts = [d - (first - HALO + r) for d in docs]
        m1[r : r + 8, :] = jnp.where(any_of([row8 == d for d in starts]), 0.0, 1.0)
        if r >= HALO:
            both = [row8 == d for d in starts] + [row8 == d + 1 for d in starts]
            m2[r - HALO : r - HALO + 8, :] = jnp.where(any_of(both), 0.0, 1.0)
    t_at = iota((L, L), 0)
    s_at = iota((L, L), 1)

    small[2].wait()
    small[3].wait()
    small[4].wait()

    def conv_half(q, block, before, taps):
        ext = jnp.concatenate([before, block], axis=0).astype(F32)
        mask1 = m1[q * L : q * L + HALO + L, :]
        mask2 = m2[q * L : (q + 1) * L, :]
        ext1 = pltpu.roll(ext, 1, 0) * jnp.concatenate([mask1, mask1], axis=1)
        near = taps[0:1, :] * ext[HALO:] + taps[1:2, :] * ext1[HALO:]
        far = taps[2:3, :] * ext[8:] + taps[3:4, :] * ext1[8:]
        far = pltpu.roll(far, 2, 0)[8:]
        return near + far * jnp.concatenate([mask2, mask2], axis=1)

    def silu_of_half(half):
        return half + half * jnp.tanh(half)

    taps_bc = cbc_ref[...].astype(F32) * 0.5

    def segment(at):
        count = 0
        for d in docs:
            count = count + jnp.where(at >= d, 1, 0)
        return count

    def shared(q, before):
        block = bcs[q * L : (q + 1) * L, :]
        both = silu_of_half(conv_half(q, block, before, taps_bc))
        b_st, c_st = both[:, :128], both[:, 128:]
        begin = first + q * L
        seg_t, seg_s = segment(t_at + begin), segment(iota((1, L), 1) + begin)
        scores = dot(c_st.astype(BF16), b_st.astype(BF16), NT)
        ok = (s_at <= t_at) & (seg_t == seg_s)
        gbm[q, 0:L, :] = jnp.where(ok, scores, 0.0).astype(BF16)
        b_kept = jnp.where(seg_t == segment(begin + L - 1), b_st, 0.0)
        gbm[q, L : 2 * L, :] = jnp.transpose(b_kept).astype(BF16)
        com[q] = jnp.where(seg_t == segment(begin - 1), c_st, 0.0).astype(BF16)
        cam[q * L : (q + 1) * L, :] = jnp.where(seg_t == segment(first - 1), c_st, 0.0).astype(BF16)

    for q in range(1, chunks):
        shared(q, bcs[q * L - HALO : q * L, :])

    @pl.when(me == 0)
    def _():
        xh[...] = jnp.zeros_like(xh)
        bch[...] = jnp.zeros_like(bch)

    @pl.when(me > 0)
    def _():
        for copy in halo_copies():
            copy.wait_recv()

    shared(0, bch[...])

    def exchange_copy(t):
        at = pl.ds(t * per_tile, per_tile)
        return pltpu.make_async_remote_copy(
            src_ref=sp.at[at, 1 - core], dst_ref=ex.at[at], send_sem=ex_send.at[t],
            recv_sem=ex_recv.at[t], device_id={"ctx": peer}, device_id_type=MESH,
        )

    def piece_copy(p):
        return pltpu.make_async_remote_copy(
            src_ref=sc.at[p], dst_ref=rp.at[chip, lax.rem(p, ppc)], send_sem=send1.at[p],
            recv_sem=recv1.at[chip * ppc + lax.rem(p, ppc)],
            device_id={"ctx": 2 * (p // ppc) + core}, device_id_type=MESH,
        )

    def keep_of(piece):
        return piece[64:65, :] + piece[65:66, :]

    def keep_rows(keep):
        high = keep.astype(BF16).astype(F32)
        row = iota((KROWS, keep.shape[1]), 0)
        return jnp.where(row == 0, high, jnp.where(row == 1, keep - high, 0.0)).astype(BF16)

    def both_cores(p):
        mine, other = sp[p, core].astype(F32), ex[p].astype(F32)
        return jnp.where(core == 0, mine, other), jnp.where(core == 0, other, mine)

    def give(t):
        exchange_copy(t).wait_recv()
        for j in range(per_tile):
            p = t * per_tile + j
            early, late = both_cores(p)
            sc[p, 0:64, :] = (keep_of(late) * early[0:64, :] + late[0:64, :]).astype(BF16)
            sc[p, 64 : 64 + KROWS, :] = keep_rows(keep_of(late) * keep_of(early))

            @pl.when(p // ppc != chip)
            def _():
                piece_copy(p).start()

            @pl.when(p // ppc == chip)
            def _():
                rp[chip, lax.rem(p, ppc)] = sc[p]

    def pass_a(i, carry):
        t = tile_at(i)
        x_copy(t).wait()
        taps = cx_ref[:, cols(t)].astype(F32) * 0.5
        state = jnp.zeros((128, W), F32)
        for q in range(chunks):
            at = slice(q * L, (q + 1) * L)
            block = xs[at, cols(t)]
            before = xh[:, cols(t)] if q == 0 else xs[q * L - HALO : q * L, cols(t)]
            xc = silu_of_half(conv_half(q, block, before, taps))
            xc = xc.astype(BF16)
            v = xc * xcs[at, cols(t)]
            xcs[at, cols(t)] = xc
            hs[q, :, cols(t)] = state.astype(BF16)
            both = dot(gbm[q], v)
            yl[at, cols(t)] = both[0:L, :]
            fresh = both[L:, :]
            state = (
                rowsx[q : q + 1, cols(t)] * state
                + rowsx[chunks + q : chunks + q + 1, cols(t)] * fresh
            )
        keep = rowsx[2 * chunks : 2 * chunks + 1, cols(t)]
        krows = keep_rows(keep)
        for j in range(per_tile):
            p = t * per_tile + j
            lanes = slice(j * 128, (j + 1) * 128)
            for half in range(2):
                sp[p, half, 0:64, :] = state[half * 64 : half * 64 + 64, lanes].astype(BF16)
                sp[p, half, 64 : 64 + KROWS, :] = krows[:, lanes]
        exchange_copy(t).start()

        @pl.when(i > 0)
        def _():
            give(tile_at(i - 1))

        return carry

    lax.fori_loop(0, tiles, pass_a, 0)
    give(tile_at(tiles - 1))

    def pass_b(i, carry):
        t = tile_at(i)
        z_copy(t).wait()
        etile = es[:, cols(t)]
        skip = rowsx[2 * chunks + 1 : 2 * chunks + 2, cols(t)]
        wide[...] = dot(a_s[...], etile)
        wide2[...] = dot(e_s[...], etile)
        for q in range(chunks):
            at = slice(q * L, (q + 1) * L)
            mixed = yl[at, cols(t)] + dot(com[q], hs[q, :, cols(t)])
            own = mixed * wide[at, :] + skip * xcs[at, cols(t)].astype(F32)
            gate = silu_of_half(zs[at, cols(t)].astype(F32) * 0.5)
            yl[at, cols(t)] = own * gate
            sz[at, cols(t)] = wide2[at, :] * gate
        return carry

    split_b = 3
    lax.fori_loop(0, split_b, pass_b, 0)

    def piece_in(d, k):
        return pltpu.make_async_remote_copy(
            src_ref=sc.at[0], dst_ref=rp.at[d, k], send_sem=send1.at[0],
            recv_sem=recv1.at[d * ppc + k], device_id={"ctx": peer}, device_id_type=MESH,
        )

    def enter_copy(d, k):
        return pltpu.make_async_remote_copy(
            src_ref=ap.at[d, k], dst_ref=ain.at[chip * ppc + k], send_sem=send2.at[d * ppc + k],
            recv_sem=recv2.at[chip * ppc + k], device_id={"ctx": 2 * d + core}, device_id_type=MESH,
        )

    def enter_in(p):
        return pltpu.make_async_remote_copy(
            src_ref=ap.at[0, 0], dst_ref=ain.at[p], send_sem=send2.at[0],
            recv_sem=recv2.at[p], device_id={"ctx": peer}, device_id_type=MESH,
        )

    for k in range(ppc):
        def scan(d, state):
            @pl.when(d != chip)
            def _():
                piece_in(d, k).wait_recv()

            ap[d, k] = state.astype(BF16)
            piece = rp[d, k].astype(F32)
            return keep_of(piece) * state + piece[0:64, :]

        lax.fori_loop(0, chips, scan, jnp.zeros((64, 128), F32))

        def spread(i, carry):
            enter_copy(lax.rem(chip + chips - i, chips), k).start()
            return carry

        lax.fori_loop(1, chips, spread, 0)
        ain[chip * ppc + k] = ap[chip, k]

    lax.fori_loop(split_b, tiles, pass_b, 0)

    sq[...] = jnp.zeros_like(sq)

    def forward_copy(t):
        at = pl.ds(t * per_tile, per_tile)
        return pltpu.make_async_remote_copy(
            src_ref=fw.at[at], dst_ref=ent.at[at, own_rows], send_sem=fw_send.at[t],
            recv_sem=fw_recv.at[t], device_id={"ctx": peer}, device_id_type=MESH,
        )

    def forward(t):
        for j in range(per_tile):
            p = t * per_tile + j

            @pl.when(p // ppc != chip)
            def _():
                enter_in(p).wait_recv()

            early, _ = both_cores(p)
            to_first = ain[p].astype(F32)
            to_second = keep_of(early) * to_first + early[0:64, :]
            ent[p, own_rows, :] = jnp.where(core == 0, to_first, to_second).astype(BF16)
            fw[p] = jnp.where(core == 0, to_second, to_first).astype(BF16)
        forward_copy(t).start()

    forward(tile_at(0))

    def pass_c(i, carry):
        t = tile_at(i)

        @pl.when(i + 1 < tiles)
        def _():
            forward(tile_at(i + 1))

        forward_copy(t).wait_recv()
        entering = jnp.concatenate([ent[t * per_tile + j] for j in range(per_tile)], axis=1)
        step = 2 * L
        for q in range(tokens // step):
            at = slice(q * step, (q + 1) * step)
            gated = yl[at, cols(t)] + dot(cam[at, :], entering) * sz[at, cols(t)]
            g_ref[at, cols(t)] = gated.astype(BF16)
            squares = gated * gated
            sq[at, :] += squares[:, :128] + squares[:, 128:]
        return carry

    lax.fori_loop(0, tiles, pass_c, 0)

    total = jnp.zeros((8, L), F32)
    for q in range(chunks):
        pick = jnp.where(iota((8, 128), 0) == q, 1.0, 0.0).astype(BF16)
        high, low = split2(sq[q * L : (q + 1) * L, :])
        total = total + dot(pick, high, NT) + dot(pick, low, NT)
    sqx[0] = total

    def sq_copy(i):
        return pltpu.make_async_remote_copy(
            src_ref=sqx.at[0], dst_ref=sqx.at[i], send_sem=send3.at[i - 1],
            recv_sem=recv3.at[i - 1], device_id={"head": lax.rem(my + i, y_count)},
            device_id_type=MESH,
        )

    for i in range(1, y_count):
        sq_copy(i).start()
    for i in range(1, y_count):
        sq_copy(i).wait_recv()
    whole = sqx[0]
    for i in range(1, y_count):
        whole = whole + sqx[i]
    scale = lax.rsqrt(whole * (1.0 / width_all) + 1e-05)
    for q in range(chunks):
        rx_ref[q * L : (q + 1) * L, :] = jnp.transpose(
            jnp.broadcast_to(scale[q : q + 1, :], (128, L))
        )

    for i in range(1, y_count):
        sq_copy(i).wait_send()

    @pl.when(me < n - 1)
    def _():
        for copy in halo_copies():
            copy.wait_send()

    for t in range(tiles):
        exchange_copy(t).wait_send()
        forward_copy(t).wait_send()

    def drain1(p, carry):
        @pl.when(p // ppc != chip)
        def _():
            piece_copy(p).wait_send()

        return carry

    lax.fori_loop(0, pairs, drain1, 0)
    for k in range(ppc):
        def drain2(i, carry):
            enter_copy(lax.rem(chip + chips - i, chips), k).wait_send()
            return carry

        lax.fori_loop(1, chips, drain2, 0)


def norm_kernel(g_ref, rx_ref, gain_ref, out_ref, stage, sem):
    rows, width = g_ref.shape
    block = 128
    gain = gain_ref[...].reshape(1, width).astype(F32)

    def copy(i):
        at = pl.ds(i * block, block)
        return pltpu.make_async_copy(stage.at[at, :], out_ref.at[at, :], sem.at[i])

    for i in range(rows // block):
        at = slice(i * block, (i + 1) * block)
        scale = rx_ref[at, :]
        for j in range(width // 128):
            lanes = slice(j * 128, (j + 1) * 128)
            stage[at, lanes] = (g_ref[at, lanes].astype(F32) * scale * gain[:, lanes]).astype(BF16)
        copy(i).start()
    for i in range(rows // block):
        copy(i).wait()


def per_device(
    n, y_count,
    x_raw, z_gate, bc_raw, conv_x, conv_bc, log_decay, step_size, skip_coef, norm_gain, doc_starts,
):
    tokens, width = x_raw.shape
    heads = log_decay.shape[1]
    chunks, tiles = tokens // L, width // W
    pairs, chips = width // 128, n // 2
    ppc = pairs // chips
    any_spec = pl.BlockSpec(memory_space=pl.ANY)
    vmem = pl.BlockSpec(memory_space=pltpu.VMEM)
    smem = pl.BlockSpec(memory_space=pltpu.SMEM)
    dma = pltpu.SemaphoreType.DMA
    gated, scale = pl.pallas_call(
        functools.partial(layer_kernel, n, y_count, float(width * y_count)),
        out_shape=(
            pltpu.VMEM((tokens, width), BF16),
            pltpu.VMEM((tokens, 128), F32),
        ),
        in_specs=[smem] + [any_spec] * 8,
        out_specs=(vmem, vmem),
        scratch_shapes=[
            pltpu.VMEM((tokens, width), BF16),
            pltpu.VMEM((tokens, width), BF16),
            pltpu.VMEM((tokens, 256), BF16),
            pltpu.VMEM((heads, tokens), F32),
            pltpu.VMEM((heads, tokens), F32),
            pltpu.VMEM((4, width), BF16),
            pltpu.VMEM((4, 256), BF16),
            pltpu.VMEM((1, heads), F32),
            pltpu.VMEM((HALO, width), BF16),
            pltpu.VMEM((HALO, 256), BF16),
            pltpu.VMEM((2 * heads, width), BF16),
            pltpu.VMEM((HALO + tokens, 128), F32),
            pltpu.VMEM((tokens, 128), F32),
            pltpu.VMEM((chunks, 2 * L, L), BF16),
            pltpu.VMEM((chunks, L, 128), BF16),
            pltpu.VMEM((tokens, 128), BF16),
            pltpu.VMEM((tokens, 2 * heads), BF16),
            pltpu.VMEM((tokens, 2 * heads), BF16),
            pltpu.VMEM((tokens, 2 * heads), BF16),
            pltpu.VMEM((32, heads), F32),
            pltpu.VMEM((32, width), F32),
            pltpu.VMEM((tokens, width), BF16),
            pltpu.VMEM((chunks, 128, width), BF16),
            pltpu.VMEM((tokens, width), F32),
            pltpu.VMEM((tokens, width), F32),
            pltpu.VMEM((tokens, W), F32),
            pltpu.VMEM((tokens, W), F32),
            pltpu.VMEM((pairs, 2, 64 + KROWS, 128), BF16),
            pltpu.VMEM((pairs, 64 + KROWS, 128), BF16),
            pltpu.VMEM((pairs, 64 + KROWS, 128), BF16),
            pltpu.VMEM((chips, ppc, 64 + KROWS, 128), BF16),
            pltpu.VMEM((chips, ppc, 64, 128), BF16),
            pltpu.VMEM((pairs, 64, 128), BF16),
            pltpu.VMEM((pairs, 64, 128), BF16),
            pltpu.VMEM((pairs, 128, 128), BF16),
            pltpu.VMEM((tokens, 128), F32),
            pltpu.VMEM((y_count, 8, 128), F32),
            dma((6,)), dma((tiles,)), dma((tiles,)), dma((2,)), dma((2,)),
            dma((tiles,)), dma((tiles,)), dma((pairs,)), dma((pairs,)), dma((pairs,)), dma((pairs,)),
            dma((tiles,)), dma((tiles,)),
            dma((y_count,)), dma((y_count,)),
        ],
        compiler_params=pltpu.CompilerParams(
            collective_id=0, has_side_effects=True, vmem_limit_bytes=59 * 1024 * 1024
        ),
        name="layer",
    )(
        doc_starts, x_raw, z_gate, bc_raw, log_decay.T, step_size.T, conv_x, conv_bc,
        skip_coef.reshape(1, heads),
    )
    return pl.pallas_call(
        norm_kernel,
        out_shape=jax.ShapeDtypeStruct((tokens, width), BF16),
        in_specs=[vmem] * 3,
        out_specs=any_spec,
        scratch_shapes=[pltpu.VMEM((tokens, width), BF16), dma((tokens // 128,))],
        compiler_params=pltpu.CompilerParams(vmem_limit_bytes=16 * 1024 * 1024),
        name="norm",
    )(gated, scale, norm_gain)


def solution(mesh):
    in_specs = (
        P("ctx", "head"),
        P("ctx", "head"),
        P("ctx", None),
        P(None, "head"),
        P(),
        P("ctx", "head"),
        P("ctx", "head"),
        P("head"),
        P("head"),
        P(),
    )
    return jax.shard_map(
        functools.partial(per_device, mesh.shape["ctx"], mesh.shape["head"]),
        mesh=mesh, in_specs=in_specs, out_specs=P("ctx", "head"), check_vma=False,
    )
```

```python
import functools

import jax
import jax.numpy as jnp
from jax import lax
from jax.experimental import pallas as pl
from jax.experimental.pallas import tpu as pltpu
from jax.sharding import PartitionSpec as P

MESH = pl.DeviceIdType.MESH
F32, BF16 = jnp.float32, jnp.bfloat16
L = 128
W = 256
UNROLL = 1
HALO = 16
KROWS = 16
NN = (((1,), (0,)), ((), ()))
NT = (((1,), (1,)), ((), ()))


def dot(a, b, dims=NN, precision=None):
    return lax.dot_general(a, b, dims, precision=precision, preferred_element_type=F32)


def iota(shape, dim):
    return lax.broadcasted_iota(jnp.int32, shape, dim)


def split2(value):
    high = value.astype(BF16)
    return high, (value - high.astype(F32)).astype(BF16)


def layer_kernel(
    n, y_count, width_all,
    docs_hbm, x_ref, z_ref, bc_ref, ld_ref, st_ref, cx_hbm, cbc_hbm, skip_hbm,
    g_ref, rx_ref,
    docs_ref, xs, zs, bcs, lds, sts, cx_ref, cbc_ref, skip_ref, xh, bch, es, m1, m2, gbm, com, cam, a_s, b_s, e_s, rows, rowsx,
    xcs, hs, yl, sz, wide, wide2, sp, ex, sc, rp, ap, ain, fw, ent, sq, sqx,
    load_sem, x_sem, z_sem, halo_send, halo_recv, ex_send, ex_recv, send1, recv1, send2, recv2,
    fw_send, fw_recv, send3, recv3,
):
    me = lax.axis_index("ctx")
    my = lax.axis_index("head")
    tokens, width = x_ref.shape
    heads = ld_ref.shape[0]
    chunks, tiles = tokens // L, width // W
    pairs = width // 128
    per_tile = W // 128
    chips = n // 2
    ppc = pairs // chips
    chip, core = me // 2, lax.rem(me, 2)
    peer = me + 1 - 2 * core
    own_rows = pl.ds(pl.multiple_of(core * 64, 64), 64)
    hd = width // heads
    first = me * tokens
    tile0 = lax.rem(chip * tiles // chips, tiles)

    def tile_at(i):
        return lax.rem(tile0 + i, tiles)

    def cols(t):
        return pl.ds(pl.multiple_of(t * W, W), W)

    def x_copy(t):
        return pltpu.make_async_copy(x_ref.at[:, cols(t)], xs.at[:, cols(t)], x_sem.at[t])

    def z_copy(t):
        return pltpu.make_async_copy(z_ref.at[:, cols(t)], zs.at[:, cols(t)], z_sem.at[t])

    barrier = pltpu.get_barrier_semaphore()

    def greet(device):
        pl.semaphore_signal(barrier, inc=1, device_id=device, device_id_type=MESH)

    greet({"ctx": peer})
    greet({"ctx": lax.rem(me + n - 1 + 2 * core, n)})
    for i in range(1, chips):
        greet({"ctx": lax.rem(me + 2 * i, n)})
    for i in range(1, y_count):
        greet({"head": lax.rem(my + i, y_count)})

    small = [
        pltpu.make_async_copy(docs_hbm, docs_ref, load_sem.at[6]),
        pltpu.make_async_copy(ld_ref, lds, load_sem.at[0]),
        pltpu.make_async_copy(st_ref, sts, load_sem.at[1]),
        pltpu.make_async_copy(bc_ref, bcs, load_sem.at[2]),
        pltpu.make_async_copy(cx_hbm, cx_ref, load_sem.at[3]),
        pltpu.make_async_copy(cbc_hbm, cbc_ref, load_sem.at[4]),
        pltpu.make_async_copy(skip_hbm, skip_ref, load_sem.at[5]),
    ]
    for copy in small:
        copy.start()
    for i in range(tiles):
        x_copy(tile_at(i)).start()
    for i in range(tiles):
        z_copy(tile_at(i)).start()

    es[...] = jnp.where(
        (iota((2 * heads, width), 1) // hd) == (iota((2 * heads, width), 0) & (heads - 1)), 1.0, 0.0
    ).astype(BF16)

    small[0].wait()
    docs = [docs_ref[i] for i in range(docs_ref.shape[0])]

    def crossed(low, high):
        hit = None
        for d in docs:
            one = (d > low) & (d <= high)
            hit = one if hit is None else hit | one
        return hit

    def put2(ref, value):
        high = value.astype(BF16).astype(F32)
        low = value - high
        for q in range(chunks):
            at = slice(q * heads, (q + 1) * heads)
            both = jnp.concatenate([high[at], low[at]], axis=0)
            ref[q * L : (q + 1) * L, :] = jnp.transpose(both).astype(BF16)

    def any_of(conditions):
        hit = conditions[0]
        for one in conditions[1:]:
            hit = hit | one
        return hit

    row8 = iota((8, 128), 0)
    for r in range(0, HALO + tokens, 8):
        starts = [d - (first - HALO + r) for d in docs]
        m1[r : r + 8, :] = jnp.where(any_of([row8 == d for d in starts]), 0.0, 1.0)
        if r >= HALO:
            both = [row8 == d for d in starts] + [row8 == d + 1 for d in starts]
            m2[r - HALO : r - HALO + 8, :] = jnp.where(any_of(both), 0.0, 1.0)
    small[1].wait()
    small[2].wait()
    small[6].wait()
    tri = jnp.where(iota((L, L), 0) <= iota((L, L), 1), 1.0, 0.0).astype(BF16)
    ld = jnp.concatenate([lds[:, q * L : (q + 1) * L] for q in range(chunks)], axis=0)
    st = jnp.concatenate([sts[:, q * L : (q + 1) * L] for q in range(chunks)], axis=0)
    high, mid = split2(ld)
    low = (ld - high.astype(F32) - mid.astype(F32)).astype(BF16)
    sums = dot(jnp.concatenate([high, mid, low], axis=0), tri)
    rows_all = chunks * heads
    lc = sums[0:rows_all] + (sums[rows_all : 2 * rows_all] + sums[2 * rows_all :])
    center, end = lc[:, L // 2 : L // 2 + 1], lc[:, L - 1 : L]
    bases = [jnp.zeros((heads, 1), F32)]
    for q in range(chunks):
        bases.append(bases[-1] + end[q * heads : (q + 1) * heads])
    base = bases[-1]
    put2(a_s, jnp.exp(lc - center))
    put2(b_s, jnp.exp(center - lc) * st)
    put2(e_s, jnp.exp(jnp.concatenate(bases[:-1], axis=0) + lc))
    centers = [center[q * heads : (q + 1) * heads] for q in range(chunks)]
    ends = [end[q * heads : (q + 1) * heads] for q in range(chunks)]

    pl.semaphore_wait(barrier, chips + 1 + y_count - 1)

    def halo_copies():
        to = {"ctx": lax.rem(me + 1, n)}
        tail = pl.ds(tokens - HALO, HALO)
        return (
            pltpu.make_async_remote_copy(
                src_ref=x_ref.at[tail, :], dst_ref=xh, send_sem=halo_send.at[0],
                recv_sem=halo_recv.at[0], device_id=to, device_id_type=MESH,
            ),
            pltpu.make_async_remote_copy(
                src_ref=bc_ref.at[tail, :], dst_ref=bch, send_sem=halo_send.at[1],
                recv_sem=halo_recv.at[1], device_id=to, device_id_type=MESH,
            ),
        )

    @pl.when(me < n - 1)
    def _():
        for copy in halo_copies():
            copy.start()

    lane = iota((heads, 128), 1)
    table = jnp.zeros((heads, 128), F32)
    for q in range(chunks):
        later = centers[q + 1] if q + 1 < chunks else jnp.zeros((heads, 1), F32)
        k = jnp.exp(ends[q] - centers[q] + later)
        b = jnp.full((heads, 1), first + q * L, jnp.int32)
        table = jnp.where(lane == q, jnp.where(crossed(b - 1, b + (L - 1)), 0.0, k), table)
        table = jnp.where(lane == chunks + q, k, table)
    b = jnp.full((heads, 1), first, jnp.int32)
    keep_all = jnp.where(crossed(b - 1, b + (tokens - 1)), 0.0, jnp.exp(base))
    table = jnp.where(lane == 2 * chunks, keep_all, table)
    rows[...] = jnp.transpose(table)[0:32, :]
    rows[2 * chunks + 1 : 2 * chunks + 2, :] = skip_ref[...]
    r_high, r_low = split2(rows[...])
    rowsx[...] = dot(r_high, es[0:heads, :]) + dot(r_low, es[0:heads, :])

    def expand_b(i, carry):
        at = pl.ds(pl.multiple_of(i * 512, 512), 512)
        xcs[:, at] = dot(b_s[...], es[:, at]).astype(BF16)
        return carry

    lax.fori_loop(0, width // 512, expand_b, 0)

    t_at = iota((L, L), 0)
    s_at = iota((L, L), 1)

    small[3].wait()
    small[4].wait()
    small[5].wait()

    def conv_half(q, block, before, taps):
        ext = jnp.concatenate([before, block], axis=0).astype(F32)
        mask1 = m1[q * L : q * L + HALO + L, :]
        mask2 = m2[q * L : (q + 1) * L, :]
        ext1 = pltpu.roll(ext, 1, 0) * jnp.concatenate([mask1, mask1], axis=1)
        near = taps[0:1, :] * ext[HALO:] + taps[1:2, :] * ext1[HALO:]
        far = taps[2:3, :] * ext[8:] + taps[3:4, :] * ext1[8:]
        far = pltpu.roll(far, 2, 0)[8:]
        return near + far * jnp.concatenate([mask2, mask2], axis=1)

    def silu_of_half(half):
        return half + half * jnp.tanh(half)

    taps_bc = cbc_ref[...].astype(F32) * 0.5

    def segment(at):
        count = 0
        for d in docs:
            count = count + jnp.where(at >= d, 1, 0)
        return count

    def shared(q, before):
        block = bcs[q * L : (q + 1) * L, :]
        both = silu_of_half(conv_half(q, block, before, taps_bc))
        b_st, c_st = both[:, :128], both[:, 128:]
        begin = first + q * L
        seg_t, seg_s = segment(t_at + begin), segment(iota((1, L), 1) + begin)
        scores = dot(c_st.astype(BF16), b_st.astype(BF16), NT)
        ok = (s_at <= t_at) & (seg_t == seg_s)
        gbm[q, 0:L, :] = jnp.where(ok, scores, 0.0).astype(BF16)
        b_kept = jnp.where(seg_t == segment(begin + L - 1), b_st, 0.0)
        gbm[q, L : 2 * L, :] = jnp.transpose(b_kept).astype(BF16)
        com[q] = jnp.where(seg_t == segment(begin - 1), c_st, 0.0).astype(BF16)
        cam[q * L : (q + 1) * L, :] = jnp.where(seg_t == segment(first - 1), c_st, 0.0).astype(BF16)

    for q in range(1, chunks):
        shared(q, bcs[q * L - HALO : q * L, :])

    @pl.when(me == 0)
    def _():
        xh[...] = jnp.zeros_like(xh)
        bch[...] = jnp.zeros_like(bch)

    @pl.when(me > 0)
    def _():
        for copy in halo_copies():
            copy.wait_recv()

    shared(0, bch[...])

    def exchange_copy(t):
        at = pl.ds(t * per_tile, per_tile)
        return pltpu.make_async_remote_copy(
            src_ref=sp.at[at, 1 - core], dst_ref=ex.at[at], send_sem=ex_send.at[t],
            recv_sem=ex_recv.at[t], device_id={"ctx": peer}, device_id_type=MESH,
        )

    def piece_copy(p):
        return pltpu.make_async_remote_copy(
            src_ref=sc.at[p], dst_ref=rp.at[chip, lax.rem(p, ppc)], send_sem=send1.at[p],
            recv_sem=recv1.at[chip * ppc + lax.rem(p, ppc)],
            device_id={"ctx": 2 * (p // ppc) + core}, device_id_type=MESH,
        )

    def keep_of(piece):
        return piece[64:65, :] + piece[65:66, :]

    def keep_rows(keep):
        high = keep.astype(BF16).astype(F32)
        row = iota((KROWS, keep.shape[1]), 0)
        return jnp.where(row == 0, high, jnp.where(row == 1, keep - high, 0.0)).astype(BF16)

    def both_cores(p):
        mine, other = sp[p, core].astype(F32), ex[p].astype(F32)
        return jnp.where(core == 0, mine, other), jnp.where(core == 0, other, mine)

    def give(t):
        exchange_copy(t).wait_recv()
        for j in range(per_tile):
            p = t * per_tile + j
            early, late = both_cores(p)
            sc[p, 0:64, :] = (keep_of(late) * early[0:64, :] + late[0:64, :]).astype(BF16)
            sc[p, 64 : 64 + KROWS, :] = keep_rows(keep_of(late) * keep_of(early))

            @pl.when(p // ppc != chip)
            def _():
                piece_copy(p).start()

            @pl.when(p // ppc == chip)
            def _():
                rp[chip, lax.rem(p, ppc)] = sc[p]

    def tile_a(t):
        x_copy(t).wait()
        taps = cx_ref[:, cols(t)].astype(F32) * 0.5
        state = jnp.zeros((128, W), F32)
        for q in range(chunks):
            at = slice(q * L, (q + 1) * L)
            block = xs[at, cols(t)]
            before = xh[:, cols(t)] if q == 0 else xs[q * L - HALO : q * L, cols(t)]
            xc = silu_of_half(conv_half(q, block, before, taps))
            xc = xc.astype(BF16)
            v = xc * xcs[at, cols(t)]
            xcs[at, cols(t)] = xc
            hs[q, :, cols(t)] = state.astype(BF16)
            both = dot(gbm[q], v)
            yl[at, cols(t)] = both[0:L, :]
            fresh = both[L:, :]
            state = (
                rowsx[q : q + 1, cols(t)] * state
                + rowsx[chunks + q : chunks + q + 1, cols(t)] * fresh
            )
        keep = rowsx[2 * chunks : 2 * chunks + 1, cols(t)]
        krows = keep_rows(keep)
        for j in range(per_tile):
            p = t * per_tile + j
            lanes = slice(j * 128, (j + 1) * 128)
            for half in range(2):
                sp[p, half, 0:64, :] = state[half * 64 : half * 64 + 64, lanes].astype(BF16)
                sp[p, half, 64 : 64 + KROWS, :] = krows[:, lanes]

    def pass_a(i, carry):
        at = [tile_at(UNROLL * i + j) for j in range(UNROLL)]
        for t in at:
            tile_a(t)
        for t in at:
            exchange_copy(t).start()

        @pl.when(i > 0)
        def _():
            for j in range(UNROLL):
                give(tile_at(UNROLL * (i - 1) + j))

        return carry

    lax.fori_loop(0, tiles // UNROLL, pass_a, 0)

    def pass_b(i, carry):
        t = tile_at(i)
        z_copy(t).wait()
        etile = es[:, cols(t)]
        skip = rowsx[2 * chunks + 1 : 2 * chunks + 2, cols(t)]
        wide[...] = dot(a_s[...], etile)
        wide2[...] = dot(e_s[...], etile)
        for q in range(chunks):
            at = slice(q * L, (q + 1) * L)
            mixed = yl[at, cols(t)] + dot(com[q], hs[q, :, cols(t)])
            own = mixed * wide[at, :] + skip * xcs[at, cols(t)].astype(F32)
            gate = silu_of_half(zs[at, cols(t)].astype(F32) * 0.5)
            yl[at, cols(t)] = own * gate
            sz[at, cols(t)] = wide2[at, :] * gate
        return carry

    lax.fori_loop(0, 1, pass_b, 0)
    for j in range(UNROLL):
        give(tile_at(tiles - UNROLL + j))
    split_b = 3
    lax.fori_loop(1, split_b, pass_b, 0)

    def piece_in(d, k):
        return pltpu.make_async_remote_copy(
            src_ref=sc.at[0], dst_ref=rp.at[d, k], send_sem=send1.at[0],
            recv_sem=recv1.at[d * ppc + k], device_id={"ctx": peer}, device_id_type=MESH,
        )

    def enter_copy(d, k):
        return pltpu.make_async_remote_copy(
            src_ref=ap.at[d, k], dst_ref=ain.at[chip * ppc + k], send_sem=send2.at[d * ppc + k],
            recv_sem=recv2.at[chip * ppc + k], device_id={"ctx": 2 * d + core}, device_id_type=MESH,
        )

    def enter_in(p):
        return pltpu.make_async_remote_copy(
            src_ref=ap.at[0, 0], dst_ref=ain.at[p], send_sem=send2.at[0],
            recv_sem=recv2.at[p], device_id={"ctx": peer}, device_id_type=MESH,
        )

    for k in range(ppc):
        for d in range(chips):
            @pl.when(d != chip)
            def _():
                piece_in(d, k).wait_recv()

        state = jnp.zeros((64, 128), F32)
        for d in range(chips):
            ap[d, k] = state.astype(BF16)
            piece = rp[d, k].astype(F32)
            state = keep_of(piece) * state + piece[0:64, :]

        def spread(i, carry):
            enter_copy(lax.rem(chip + chips - i, chips), k).start()
            return carry

        lax.fori_loop(1, chips, spread, 0)
        ain[chip * ppc + k] = ap[chip, k]

    lax.fori_loop(split_b, tiles, pass_b, 0)

    sq[...] = jnp.zeros_like(sq)

    def forward_copy(t):
        at = pl.ds(t * per_tile, per_tile)
        return pltpu.make_async_remote_copy(
            src_ref=fw.at[at], dst_ref=ent.at[at, own_rows], send_sem=fw_send.at[t],
            recv_sem=fw_recv.at[t], device_id={"ctx": peer}, device_id_type=MESH,
        )

    def forward(t):
        for j in range(per_tile):
            p = t * per_tile + j

            @pl.when(p // ppc != chip)
            def _():
                enter_in(p).wait_recv()

            early, _ = both_cores(p)
            to_first = ain[p].astype(F32)
            to_second = keep_of(early) * to_first + early[0:64, :]
            ent[p, own_rows, :] = jnp.where(core == 0, to_first, to_second).astype(BF16)
            fw[p] = jnp.where(core == 0, to_second, to_first).astype(BF16)
        forward_copy(t).start()

    for j in range(UNROLL):
        forward(tile_at(j))

    def tile_c(t):
        entering = jnp.concatenate([ent[t * per_tile + j] for j in range(per_tile)], axis=1)
        step = 2 * L
        for q in range(tokens // step):
            at = slice(q * step, (q + 1) * step)
            gated = yl[at, cols(t)] + dot(cam[at, :], entering) * sz[at, cols(t)]
            g_ref[at, cols(t)] = gated.astype(BF16)
            squares = gated * gated
            sq[at, :] += squares[:, :128] + squares[:, 128:]

    def pass_c(i, carry):
        for j in range(UNROLL):
            @pl.when(UNROLL * (i + 1) + j < tiles)
            def _():
                forward(tile_at(UNROLL * (i + 1) + j))

        at = [tile_at(UNROLL * i + j) for j in range(UNROLL)]
        for t in at:
            forward_copy(t).wait_recv()
        for t in at:
            tile_c(t)
        return carry

    lax.fori_loop(0, tiles // UNROLL, pass_c, 0)

    total = jnp.zeros((8, L), F32)
    for q in range(chunks):
        pick = jnp.where(iota((8, 128), 0) == q, 1.0, 0.0).astype(BF16)
        high, low = split2(sq[q * L : (q + 1) * L, :])
        total = total + dot(pick, high, NT) + dot(pick, low, NT)
    sqx[0] = total

    def sq_copy(i):
        return pltpu.make_async_remote_copy(
            src_ref=sqx.at[0], dst_ref=sqx.at[i], send_sem=send3.at[i - 1],
            recv_sem=recv3.at[i - 1], device_id={"head": lax.rem(my + i, y_count)},
            device_id_type=MESH,
        )

    for i in range(1, y_count):
        sq_copy(i).start()
    for i in range(1, y_count):
        sq_copy(i).wait_recv()
    whole = sqx[0]
    for i in range(1, y_count):
        whole = whole + sqx[i]
    scale = lax.rsqrt(whole * (1.0 / width_all) + 1e-05)
    for q in range(chunks):
        rx_ref[q * L : (q + 1) * L, :] = jnp.transpose(
            jnp.broadcast_to(scale[q : q + 1, :], (128, L))
        )

    for i in range(1, y_count):
        sq_copy(i).wait_send()

    @pl.when(me < n - 1)
    def _():
        for copy in halo_copies():
            copy.wait_send()

    for t in range(tiles):
        exchange_copy(t).wait_send()
        forward_copy(t).wait_send()

    def drain1(p, carry):
        @pl.when(p // ppc != chip)
        def _():
            piece_copy(p).wait_send()

        return carry

    lax.fori_loop(0, pairs, drain1, 0)
    for k in range(ppc):
        def drain2(i, carry):
            enter_copy(lax.rem(chip + chips - i, chips), k).wait_send()
            return carry

        lax.fori_loop(1, chips, drain2, 0)


def norm_kernel(g_ref, rx_ref, gain_ref, out_ref, stage, sem):
    rows, width = g_ref.shape
    block = 128
    gain = gain_ref[...].reshape(1, width).astype(F32)

    def copy(i):
        at = pl.ds(i * block, block)
        return pltpu.make_async_copy(stage.at[at, :], out_ref.at[at, :], sem.at[i])

    for i in range(rows // block):
        at = slice(i * block, (i + 1) * block)
        scale = rx_ref[at, :]
        for j in range(width // 128):
            lanes = slice(j * 128, (j + 1) * 128)
            stage[at, lanes] = (g_ref[at, lanes].astype(F32) * scale * gain[:, lanes]).astype(BF16)
        copy(i).start()
    for i in range(rows // block):
        copy(i).wait()


def per_device(
    n, y_count,
    x_raw, z_gate, bc_raw, conv_x, conv_bc, log_decay, step_size, skip_coef, norm_gain, doc_starts,
):
    tokens, width = x_raw.shape
    heads = log_decay.shape[1]
    chunks, tiles = tokens // L, width // W
    pairs, chips = width // 128, n // 2
    ppc = pairs // chips
    any_spec = pl.BlockSpec(memory_space=pl.ANY)
    vmem = pl.BlockSpec(memory_space=pltpu.VMEM)
    dma = pltpu.SemaphoreType.DMA
    gated, scale = pl.pallas_call(
        functools.partial(layer_kernel, n, y_count, float(width * y_count)),
        out_shape=(
            pltpu.VMEM((tokens, width), BF16),
            pltpu.VMEM((tokens, 128), F32),
        ),
        in_specs=[any_spec] * 9,
        out_specs=(vmem, vmem),
        scratch_shapes=[
            pltpu.SMEM(doc_starts.shape, jnp.int32),
            pltpu.VMEM((tokens, width), BF16),
            pltpu.VMEM((tokens, width), BF16),
            pltpu.VMEM((tokens, 256), BF16),
            pltpu.VMEM((heads, tokens), F32),
            pltpu.VMEM((heads, tokens), F32),
            pltpu.VMEM((4, width), BF16),
            pltpu.VMEM((4, 256), BF16),
            pltpu.VMEM((1, heads), F32),
            pltpu.VMEM((HALO, width), BF16),
            pltpu.VMEM((HALO, 256), BF16),
            pltpu.VMEM((2 * heads, width), BF16),
            pltpu.VMEM((HALO + tokens, 128), F32),
            pltpu.VMEM((tokens, 128), F32),
            pltpu.VMEM((chunks, 2 * L, L), BF16),
            pltpu.VMEM((chunks, L, 128), BF16),
            pltpu.VMEM((tokens, 128), BF16),
            pltpu.VMEM((tokens, 2 * heads), BF16),
            pltpu.VMEM((tokens, 2 * heads), BF16),
            pltpu.VMEM((tokens, 2 * heads), BF16),
            pltpu.VMEM((32, heads), F32),
            pltpu.VMEM((32, width), F32),
            pltpu.VMEM((tokens, width), BF16),
            pltpu.VMEM((chunks, 128, width), BF16),
            pltpu.VMEM((tokens, width), F32),
            pltpu.VMEM((tokens, width), F32),
            pltpu.VMEM((tokens, W), F32),
            pltpu.VMEM((tokens, W), F32),
            pltpu.VMEM((pairs, 2, 64 + KROWS, 128), BF16),
            pltpu.VMEM((pairs, 64 + KROWS, 128), BF16),
            pltpu.VMEM((pairs, 64 + KROWS, 128), BF16),
            pltpu.VMEM((chips, ppc, 64 + KROWS, 128), BF16),
            pltpu.VMEM((chips, ppc, 64, 128), BF16),
            pltpu.VMEM((pairs, 64, 128), BF16),
            pltpu.VMEM((pairs, 64, 128), BF16),
            pltpu.VMEM((pairs, 128, 128), BF16),
            pltpu.VMEM((tokens, 128), F32),
            pltpu.VMEM((y_count, 8, 128), F32),
            dma((7,)), dma((tiles,)), dma((tiles,)), dma((2,)), dma((2,)),
            dma((tiles,)), dma((tiles,)), dma((pairs,)), dma((pairs,)), dma((pairs,)), dma((pairs,)),
            dma((tiles,)), dma((tiles,)),
            dma((y_count,)), dma((y_count,)),
        ],
        compiler_params=pltpu.CompilerParams(
            collective_id=0, has_side_effects=True, vmem_limit_bytes=59 * 1024 * 1024
        ),
        name="layer",
    )(
        doc_starts, x_raw, z_gate, bc_raw, log_decay.T, step_size.T, conv_x, conv_bc,
        skip_coef.reshape(1, heads),
    )
    return pl.pallas_call(
        norm_kernel,
        out_shape=jax.ShapeDtypeStruct((tokens, width), BF16),
        in_specs=[vmem] * 3,
        out_specs=any_spec,
        scratch_shapes=[pltpu.VMEM((tokens, width), BF16), dma((tokens // 128,))],
        compiler_params=pltpu.CompilerParams(vmem_limit_bytes=16 * 1024 * 1024),
        name="norm",
    )(gated, scale, norm_gain)


def solution(mesh):
    in_specs = (
        P("ctx", "head"),
        P("ctx", "head"),
        P("ctx", None),
        P(None, "head"),
        P(),
        P("ctx", "head"),
        P("ctx", "head"),
        P("head"),
        P("head"),
        P(),
    )
    return jax.shard_map(
        functools.partial(per_device, mesh.shape["ctx"], mesh.shape["head"]),
        mesh=mesh, in_specs=in_specs, out_specs=P("ctx", "head"), check_vma=False,
    )
```

```python
import functools

import jax
import jax.numpy as jnp
from jax import lax
from jax.experimental import pallas as pl
from jax.experimental.pallas import tpu as pltpu
from jax.sharding import PartitionSpec as P

MESH = pl.DeviceIdType.MESH
F32, BF16 = jnp.float32, jnp.bfloat16
L = 128
W = 256
SECOND = 7
AHEAD = 3
UNROLL = 1
HALO = 16
KROWS = 16
NN = (((1,), (0,)), ((), ()))
NT = (((1,), (1,)), ((), ()))


def dot(a, b, dims=NN, precision=None):
    return lax.dot_general(a, b, dims, precision=precision, preferred_element_type=F32)


def iota(shape, dim):
    return lax.broadcasted_iota(jnp.int32, shape, dim)


def split2(value):
    high = value.astype(BF16)
    return high, (value - high.astype(F32)).astype(BF16)


def layer_kernel(
    n, y_count, width_all,
    docs_hbm, x_ref, z_ref, bc_ref, ld_ref, st_ref, cx_hbm, cbc_hbm, skip_hbm,
    g_ref, rx_ref,
    docs_ref, xs, zs, bcs, lds, sts, cx_ref, cbc_ref, skip_ref, xh, bch, es, m1, m2, gbm, com, cam, a_s, b_s, e_s, rows, rowsx,
    xcs, hs, yl, sz, wide, wide2, sp, ex, sc, rp, ap, ain, fw, ent, sq, sqx,
    load_sem, x_sem, z_sem, halo_send, halo_recv, ex_send, ex_recv, send1, recv1, send2, recv2,
    fw_send, fw_recv, send3, recv3,
):
    me = lax.axis_index("ctx")
    my = lax.axis_index("head")
    tokens, width = x_ref.shape
    heads = ld_ref.shape[0]
    chunks, tiles = tokens // L, width // W
    pairs = width // 128
    per_tile = W // 128
    chips = n // 2
    ppc = pairs // chips
    chip, core = me // 2, lax.rem(me, 2)
    peer = me + 1 - 2 * core
    own_rows = pl.ds(pl.multiple_of(core * 64, 64), 64)
    hd = width // heads
    first = me * tokens
    tile0 = lax.rem(chip * tiles // chips, tiles)

    def tile_at(i):
        return lax.rem(tile0 + i, tiles)

    def cols(t):
        return pl.ds(pl.multiple_of(t * W, W), W)

    def x_copy(t):
        return pltpu.make_async_copy(x_ref.at[:, cols(t)], xs.at[:, cols(t)], x_sem.at[t])

    def z_copy(t):
        return pltpu.make_async_copy(z_ref.at[:, cols(t)], zs.at[:, cols(t)], z_sem.at[t])

    barrier = pltpu.get_barrier_semaphore()

    def greet(device):
        pl.semaphore_signal(barrier, inc=1, device_id=device, device_id_type=MESH)

    greet({"ctx": peer})
    greet({"ctx": lax.rem(me + n - 1 + 2 * core, n)})
    for i in range(1, chips):
        greet({"ctx": lax.rem(me + 2 * i, n)})
    for i in range(1, y_count):
        greet({"head": lax.rem(my + i, y_count)})

    small = [
        pltpu.make_async_copy(docs_hbm, docs_ref, load_sem.at[6]),
        pltpu.make_async_copy(ld_ref, lds, load_sem.at[0]),
        pltpu.make_async_copy(st_ref, sts, load_sem.at[1]),
        pltpu.make_async_copy(bc_ref, bcs, load_sem.at[2]),
        pltpu.make_async_copy(cx_hbm, cx_ref, load_sem.at[3]),
        pltpu.make_async_copy(cbc_hbm, cbc_ref, load_sem.at[4]),
        pltpu.make_async_copy(skip_hbm, skip_ref, load_sem.at[5]),
    ]
    for copy in small:
        copy.start()
    for i in range(tiles):
        x_copy(tile_at(i)).start()
    for i in range(tiles):
        z_copy(tile_at(i)).start()

    es[...] = jnp.where(
        (iota((2 * heads, width), 1) // hd) == (iota((2 * heads, width), 0) & (heads - 1)), 1.0, 0.0
    ).astype(BF16)

    small[0].wait()
    docs = [docs_ref[i] for i in range(docs_ref.shape[0])]

    def crossed(low, high):
        hit = None
        for d in docs:
            one = (d > low) & (d <= high)
            hit = one if hit is None else hit | one
        return hit

    def put2(ref, value):
        high = value.astype(BF16).astype(F32)
        low = value - high
        for q in range(chunks):
            at = slice(q * heads, (q + 1) * heads)
            both = jnp.concatenate([high[at], low[at]], axis=0)
            ref[q * L : (q + 1) * L, :] = jnp.transpose(both).astype(BF16)

    def any_of(conditions):
        hit = conditions[0]
        for one in conditions[1:]:
            hit = hit | one
        return hit

    row8 = iota((8, 128), 0)
    for r in range(0, HALO + tokens, 8):
        starts = [d - (first - HALO + r) for d in docs]
        m1[r : r + 8, :] = jnp.where(any_of([row8 == d for d in starts]), 0.0, 1.0)
        if r >= HALO:
            both = [row8 == d for d in starts] + [row8 == d + 1 for d in starts]
            m2[r - HALO : r - HALO + 8, :] = jnp.where(any_of(both), 0.0, 1.0)
    small[1].wait()
    small[2].wait()
    small[6].wait()
    tri = jnp.where(iota((L, L), 0) <= iota((L, L), 1), 1.0, 0.0).astype(BF16)
    ld = jnp.concatenate([lds[:, q * L : (q + 1) * L] for q in range(chunks)], axis=0)
    st = jnp.concatenate([sts[:, q * L : (q + 1) * L] for q in range(chunks)], axis=0)
    high, mid = split2(ld)
    low = (ld - high.astype(F32) - mid.astype(F32)).astype(BF16)
    sums = dot(jnp.concatenate([high, mid, low], axis=0), tri)
    rows_all = chunks * heads
    lc = sums[0:rows_all] + (sums[rows_all : 2 * rows_all] + sums[2 * rows_all :])
    center, end = lc[:, L // 2 : L // 2 + 1], lc[:, L - 1 : L]
    bases = [jnp.zeros((heads, 1), F32)]
    for q in range(chunks):
        bases.append(bases[-1] + end[q * heads : (q + 1) * heads])
    base = bases[-1]
    put2(a_s, jnp.exp(lc - center))
    put2(b_s, jnp.exp(center - lc) * st)
    put2(e_s, jnp.exp(jnp.concatenate(bases[:-1], axis=0) + lc))
    centers = [center[q * heads : (q + 1) * heads] for q in range(chunks)]
    ends = [end[q * heads : (q + 1) * heads] for q in range(chunks)]

    pl.semaphore_wait(barrier, chips + 1 + y_count - 1)

    def halo_copies():
        to = {"ctx": lax.rem(me + 1, n)}
        tail = pl.ds(tokens - HALO, HALO)
        return (
            pltpu.make_async_remote_copy(
                src_ref=x_ref.at[tail, :], dst_ref=xh, send_sem=halo_send.at[0],
                recv_sem=halo_recv.at[0], device_id=to, device_id_type=MESH,
            ),
            pltpu.make_async_remote_copy(
                src_ref=bc_ref.at[tail, :], dst_ref=bch, send_sem=halo_send.at[1],
                recv_sem=halo_recv.at[1], device_id=to, device_id_type=MESH,
            ),
        )

    @pl.when(me < n - 1)
    def _():
        for copy in halo_copies():
            copy.start()

    lane = iota((heads, 128), 1)
    table = jnp.zeros((heads, 128), F32)
    for q in range(chunks):
        later = centers[q + 1] if q + 1 < chunks else jnp.zeros((heads, 1), F32)
        k = jnp.exp(ends[q] - centers[q] + later)
        b = jnp.full((heads, 1), first + q * L, jnp.int32)
        table = jnp.where(lane == q, jnp.where(crossed(b - 1, b + (L - 1)), 0.0, k), table)
        table = jnp.where(lane == chunks + q, k, table)
    b = jnp.full((heads, 1), first, jnp.int32)
    keep_all = jnp.where(crossed(b - 1, b + (tokens - 1)), 0.0, jnp.exp(base))
    table = jnp.where(lane == 2 * chunks, keep_all, table)
    rows[...] = jnp.transpose(table)[0:32, :]
    rows[2 * chunks + 1 : 2 * chunks + 2, :] = skip_ref[...]
    r_high, r_low = split2(rows[...])
    rowsx[...] = dot(r_high, es[0:heads, :]) + dot(r_low, es[0:heads, :])

    def expand_b(i, carry):
        at = pl.ds(pl.multiple_of(i * 512, 512), 512)
        xcs[:, at] = dot(b_s[...], es[:, at]).astype(BF16)
        return carry

    lax.fori_loop(0, width // 512, expand_b, 0)

    t_at = iota((L, L), 0)
    s_at = iota((L, L), 1)

    small[3].wait()
    small[4].wait()
    small[5].wait()

    def conv_half(q, block, before, taps):
        ext = jnp.concatenate([before, block], axis=0).astype(F32)
        mask1 = m1[q * L : q * L + HALO + L, :]
        mask2 = m2[q * L : (q + 1) * L, :]
        ext1 = pltpu.roll(ext, 1, 0) * jnp.concatenate([mask1, mask1], axis=1)
        near = taps[0:1, :] * ext[HALO:] + taps[1:2, :] * ext1[HALO:]
        far = taps[2:3, :] * ext[8:] + taps[3:4, :] * ext1[8:]
        far = pltpu.roll(far, 2, 0)[8:]
        return near + far * jnp.concatenate([mask2, mask2], axis=1)

    def silu_of_half(half):
        return half + half * jnp.tanh(half)

    taps_bc = cbc_ref[...].astype(F32) * 0.5

    def segment(at):
        count = 0
        for d in docs:
            count = count + jnp.where(at >= d, 1, 0)
        return count

    def shared(q, before):
        block = bcs[q * L : (q + 1) * L, :]
        both = silu_of_half(conv_half(q, block, before, taps_bc))
        b_st, c_st = both[:, :128], both[:, 128:]
        begin = first + q * L
        seg_t, seg_s = segment(t_at + begin), segment(iota((1, L), 1) + begin)
        scores = dot(c_st.astype(BF16), b_st.astype(BF16), NT)
        ok = (s_at <= t_at) & (seg_t == seg_s)
        gbm[q, 0:L, :] = jnp.where(ok, scores, 0.0).astype(BF16)
        b_kept = jnp.where(seg_t == segment(begin + L - 1), b_st, 0.0)
        gbm[q, L : 2 * L, :] = jnp.transpose(b_kept).astype(BF16)
        com[q] = jnp.where(seg_t == segment(begin - 1), c_st, 0.0).astype(BF16)
        cam[q * L : (q + 1) * L, :] = jnp.where(seg_t == segment(first - 1), c_st, 0.0).astype(BF16)

    for q in range(1, chunks):
        shared(q, bcs[q * L - HALO : q * L, :])

    @pl.when(me == 0)
    def _():
        xh[...] = jnp.zeros_like(xh)
        bch[...] = jnp.zeros_like(bch)

    @pl.when(me > 0)
    def _():
        for copy in halo_copies():
            copy.wait_recv()

    shared(0, bch[...])

    def exchange_copy(t):
        at = pl.ds(t * per_tile, per_tile)
        return pltpu.make_async_remote_copy(
            src_ref=sp.at[at, 1 - core], dst_ref=ex.at[at], send_sem=ex_send.at[t],
            recv_sem=ex_recv.at[t], device_id={"ctx": peer}, device_id_type=MESH,
        )

    def piece_copy(p):
        return pltpu.make_async_remote_copy(
            src_ref=sc.at[p], dst_ref=rp.at[chip, lax.rem(p, ppc)], send_sem=send1.at[p],
            recv_sem=recv1.at[chip * ppc + lax.rem(p, ppc)],
            device_id={"ctx": 2 * (p // ppc) + core}, device_id_type=MESH,
        )

    def keep_of(piece):
        return piece[64:65, :] + piece[65:66, :]

    def keep_rows(keep):
        high = keep.astype(BF16).astype(F32)
        row = iota((KROWS, keep.shape[1]), 0)
        return jnp.where(row == 0, high, jnp.where(row == 1, keep - high, 0.0)).astype(BF16)

    def both_cores(p):
        mine, other = sp[p, core].astype(F32), ex[p].astype(F32)
        return jnp.where(core == 0, mine, other), jnp.where(core == 0, other, mine)

    def give(t):
        exchange_copy(t).wait_recv()
        for j in range(per_tile):
            p = t * per_tile + j
            early, late = both_cores(p)
            sc[p, 0:64, :] = (keep_of(late) * early[0:64, :] + late[0:64, :]).astype(BF16)
            sc[p, 64 : 64 + KROWS, :] = keep_rows(keep_of(late) * keep_of(early))

            @pl.when(p // ppc != chip)
            def _():
                piece_copy(p).start()

            @pl.when(p // ppc == chip)
            def _():
                rp[chip, lax.rem(p, ppc)] = sc[p]

    def tile_a(t):
        x_copy(t).wait()
        taps = cx_ref[:, cols(t)].astype(F32) * 0.5
        state = jnp.zeros((128, W), F32)
        for q in range(chunks):
            at = slice(q * L, (q + 1) * L)
            block = xs[at, cols(t)]
            before = xh[:, cols(t)] if q == 0 else xs[q * L - HALO : q * L, cols(t)]
            xc = silu_of_half(conv_half(q, block, before, taps))
            xc = xc.astype(BF16)
            v = xc * xcs[at, cols(t)]
            xcs[at, cols(t)] = xc
            hs[q, :, cols(t)] = state.astype(BF16)
            both = dot(gbm[q], v)
            yl[at, cols(t)] = both[0:L, :]
            fresh = both[L:, :]
            state = (
                rowsx[q : q + 1, cols(t)] * state
                + rowsx[chunks + q : chunks + q + 1, cols(t)] * fresh
            )
        keep = rowsx[2 * chunks : 2 * chunks + 1, cols(t)]
        krows = keep_rows(keep)
        for j in range(per_tile):
            p = t * per_tile + j
            lanes = slice(j * 128, (j + 1) * 128)
            for half in range(2):
                sp[p, half, 0:64, :] = state[half * 64 : half * 64 + 64, lanes].astype(BF16)
                sp[p, half, 64 : 64 + KROWS, :] = krows[:, lanes]

    def pass_a(i, carry):
        at = [tile_at(UNROLL * i + j) for j in range(UNROLL)]
        for t in at:
            tile_a(t)
        for t in at:
            exchange_copy(t).start()

        @pl.when(i > 0)
        def _():
            for j in range(UNROLL):
                give(tile_at(UNROLL * (i - 1) + j))

        return carry

    lax.fori_loop(0, tiles // UNROLL, pass_a, 0)

    def pass_b(i, carry):
        t = tile_at(i)
        z_copy(t).wait()
        etile = es[:, cols(t)]
        skip = rowsx[2 * chunks + 1 : 2 * chunks + 2, cols(t)]
        wide[...] = dot(a_s[...], etile)
        wide2[...] = dot(e_s[...], etile)
        for q in range(chunks):
            at = slice(q * L, (q + 1) * L)
            mixed = yl[at, cols(t)] + dot(com[q], hs[q, :, cols(t)])
            own = mixed * wide[at, :] + skip * xcs[at, cols(t)].astype(F32)
            gate = silu_of_half(zs[at, cols(t)].astype(F32) * 0.5)
            yl[at, cols(t)] = own * gate
            sz[at, cols(t)] = wide2[at, :] * gate
        return carry

    lax.fori_loop(0, 1, pass_b, 0)
    for j in range(UNROLL):
        give(tile_at(tiles - UNROLL + j))
    split_b = 3
    lax.fori_loop(1, split_b, pass_b, 0)

    def piece_in(d, k):
        return pltpu.make_async_remote_copy(
            src_ref=sc.at[0], dst_ref=rp.at[d, k], send_sem=send1.at[0],
            recv_sem=recv1.at[d * ppc + k], device_id={"ctx": peer}, device_id_type=MESH,
        )

    def enter_copy(d, k):
        return pltpu.make_async_remote_copy(
            src_ref=ap.at[d, k], dst_ref=ain.at[chip * ppc + k], send_sem=send2.at[d * ppc + k],
            recv_sem=recv2.at[chip * ppc + k], device_id={"ctx": 2 * d + core}, device_id_type=MESH,
        )

    def enter_in(p):
        return pltpu.make_async_remote_copy(
            src_ref=ap.at[0, 0], dst_ref=ain.at[p], send_sem=send2.at[0],
            recv_sem=recv2.at[p], device_id={"ctx": peer}, device_id_type=MESH,
        )

    for k in range(ppc):
        for d in range(chips):
            @pl.when(d != chip)
            def _():
                piece_in(d, k).wait_recv()

        state = jnp.zeros((64, 128), F32)
        for d in range(chips):
            ap[d, k] = state.astype(BF16)
            piece = rp[d, k].astype(F32)
            state = keep_of(piece) * state + piece[0:64, :]

        def spread(i, carry):
            enter_copy(lax.rem(chip + chips - i, chips), k).start()
            return carry

        lax.fori_loop(1, chips, spread, 0)
        ain[chip * ppc + k] = ap[chip, k]


    sq[...] = jnp.zeros_like(sq)

    def forward_copy(t):
        at = pl.ds(t * per_tile, per_tile)
        return pltpu.make_async_remote_copy(
            src_ref=fw.at[at], dst_ref=ent.at[at, own_rows], send_sem=fw_send.at[t],
            recv_sem=fw_recv.at[t], device_id={"ctx": peer}, device_id_type=MESH,
        )

    def forward(t):
        for j in range(per_tile):
            p = t * per_tile + j

            @pl.when(p // ppc != chip)
            def _():
                enter_in(p).wait_recv()

            early, _ = both_cores(p)
            to_first = ain[p].astype(F32)
            to_second = keep_of(early) * to_first + early[0:64, :]
            ent[p, own_rows, :] = jnp.where(core == 0, to_first, to_second).astype(BF16)
            fw[p] = jnp.where(core == 0, to_second, to_first).astype(BF16)
        forward_copy(t).start()

    def tile_c(t):
        entering = jnp.concatenate([ent[t * per_tile + j] for j in range(per_tile)], axis=1)
        step = 2 * L
        for q in range(tokens // step):
            at = slice(q * step, (q + 1) * step)
            gated = yl[at, cols(t)] + dot(cam[at, :], entering) * sz[at, cols(t)]
            g_ref[at, cols(t)] = gated.astype(BF16)
            squares = gated * gated
            sq[at, :] += squares[:, :128] + squares[:, 128:]

    def pass_c(i, carry):
        @pl.when(i + AHEAD < tiles)
        def _():
            forward(tile_at(i + AHEAD))

        at = [tile_at(UNROLL * i + j) for j in range(UNROLL)]
        for t in at:
            forward_copy(t).wait_recv()
        for t in at:
            tile_c(t)
        return carry

    def forward_step(i, carry):
        forward(tile_at(i))
        return carry

    lax.fori_loop(split_b, SECOND, pass_b, 0)
    lax.fori_loop(0, AHEAD, forward_step, 0)
    lax.fori_loop(SECOND, tiles, pass_b, 0)
    lax.fori_loop(0, tiles // UNROLL, pass_c, 0)

    total = jnp.zeros((8, L), F32)
    for q in range(chunks):
        pick = jnp.where(iota((8, 128), 0) == q, 1.0, 0.0).astype(BF16)
        high, low = split2(sq[q * L : (q + 1) * L, :])
        total = total + dot(pick, high, NT) + dot(pick, low, NT)
    sqx[0] = total

    def sq_copy(i):
        return pltpu.make_async_remote_copy(
            src_ref=sqx.at[0], dst_ref=sqx.at[i], send_sem=send3.at[i - 1],
            recv_sem=recv3.at[i - 1], device_id={"head": lax.rem(my + i, y_count)},
            device_id_type=MESH,
        )

    for i in range(1, y_count):
        sq_copy(i).start()
    for i in range(1, y_count):
        sq_copy(i).wait_recv()
    whole = sqx[0]
    for i in range(1, y_count):
        whole = whole + sqx[i]
    scale = lax.rsqrt(whole * (1.0 / width_all) + 1e-05)
    for q in range(chunks):
        rx_ref[q * L : (q + 1) * L, :] = jnp.transpose(
            jnp.broadcast_to(scale[q : q + 1, :], (128, L))
        )

    for i in range(1, y_count):
        sq_copy(i).wait_send()

    @pl.when(me < n - 1)
    def _():
        for copy in halo_copies():
            copy.wait_send()

    for t in range(tiles):
        exchange_copy(t).wait_send()
        forward_copy(t).wait_send()

    def drain1(p, carry):
        @pl.when(p // ppc != chip)
        def _():
            piece_copy(p).wait_send()

        return carry

    lax.fori_loop(0, pairs, drain1, 0)
    for k in range(ppc):
        def drain2(i, carry):
            enter_copy(lax.rem(chip + chips - i, chips), k).wait_send()
            return carry

        lax.fori_loop(1, chips, drain2, 0)


def norm_kernel(g_ref, rx_ref, gain_ref, out_ref, stage, sem):
    rows, width = g_ref.shape
    block = 128
    gain = gain_ref[...].reshape(1, width).astype(F32)

    def copy(i):
        at = pl.ds(i * block, block)
        return pltpu.make_async_copy(stage.at[at, :], out_ref.at[at, :], sem.at[i])

    for i in range(rows // block):
        at = slice(i * block, (i + 1) * block)
        scale = rx_ref[at, :]
        for j in range(width // 128):
            lanes = slice(j * 128, (j + 1) * 128)
            stage[at, lanes] = (g_ref[at, lanes].astype(F32) * scale * gain[:, lanes]).astype(BF16)
        copy(i).start()
    for i in range(rows // block):
        copy(i).wait()


def per_device(
    n, y_count,
    x_raw, z_gate, bc_raw, conv_x, conv_bc, log_decay, step_size, skip_coef, norm_gain, doc_starts,
):
    tokens, width = x_raw.shape
    heads = log_decay.shape[1]
    chunks, tiles = tokens // L, width // W
    pairs, chips = width // 128, n // 2
    ppc = pairs // chips
    any_spec = pl.BlockSpec(memory_space=pl.ANY)
    vmem = pl.BlockSpec(memory_space=pltpu.VMEM)
    dma = pltpu.SemaphoreType.DMA
    gated, scale = pl.pallas_call(
        functools.partial(layer_kernel, n, y_count, float(width * y_count)),
        out_shape=(
            pltpu.VMEM((tokens, width), BF16),
            pltpu.VMEM((tokens, 128), F32),
        ),
        in_specs=[any_spec] * 9,
        out_specs=(vmem, vmem),
        scratch_shapes=[
            pltpu.SMEM(doc_starts.shape, jnp.int32),
            pltpu.VMEM((tokens, width), BF16),
            pltpu.VMEM((tokens, width), BF16),
            pltpu.VMEM((tokens, 256), BF16),
            pltpu.VMEM((heads, tokens), F32),
            pltpu.VMEM((heads, tokens), F32),
            pltpu.VMEM((4, width), BF16),
            pltpu.VMEM((4, 256), BF16),
            pltpu.VMEM((1, heads), F32),
            pltpu.VMEM((HALO, width), BF16),
            pltpu.VMEM((HALO, 256), BF16),
            pltpu.VMEM((2 * heads, width), BF16),
            pltpu.VMEM((HALO + tokens, 128), F32),
            pltpu.VMEM((tokens, 128), F32),
            pltpu.VMEM((chunks, 2 * L, L), BF16),
            pltpu.VMEM((chunks, L, 128), BF16),
            pltpu.VMEM((tokens, 128), BF16),
            pltpu.VMEM((tokens, 2 * heads), BF16),
            pltpu.VMEM((tokens, 2 * heads), BF16),
            pltpu.VMEM((tokens, 2 * heads), BF16),
            pltpu.VMEM((32, heads), F32),
            pltpu.VMEM((32, width), F32),
            pltpu.VMEM((tokens, width), BF16),
            pltpu.VMEM((chunks, 128, width), BF16),
            pltpu.VMEM((tokens, width), F32),
            pltpu.VMEM((tokens, width), F32),
            pltpu.VMEM((tokens, W), F32),
            pltpu.VMEM((tokens, W), F32),
            pltpu.VMEM((pairs, 2, 64 + KROWS, 128), BF16),
            pltpu.VMEM((pairs, 64 + KROWS, 128), BF16),
            pltpu.VMEM((pairs, 64 + KROWS, 128), BF16),
            pltpu.VMEM((chips, ppc, 64 + KROWS, 128), BF16),
            pltpu.VMEM((chips, ppc, 64, 128), BF16),
            pltpu.VMEM((pairs, 64, 128), BF16),
            pltpu.VMEM((pairs, 64, 128), BF16),
            pltpu.VMEM((pairs, 128, 128), BF16),
            pltpu.VMEM((tokens, 128), F32),
            pltpu.VMEM((y_count, 8, 128), F32),
            dma((7,)), dma((tiles,)), dma((tiles,)), dma((2,)), dma((2,)),
            dma((tiles,)), dma((tiles,)), dma((pairs,)), dma((pairs,)), dma((pairs,)), dma((pairs,)),
            dma((tiles,)), dma((tiles,)),
            dma((y_count,)), dma((y_count,)),
        ],
        compiler_params=pltpu.CompilerParams(
            collective_id=0, has_side_effects=True, vmem_limit_bytes=59 * 1024 * 1024
        ),
        name="layer",
    )(
        doc_starts, x_raw, z_gate, bc_raw, log_decay.T, step_size.T, conv_x, conv_bc,
        skip_coef.reshape(1, heads),
    )
    return pl.pallas_call(
        norm_kernel,
        out_shape=jax.ShapeDtypeStruct((tokens, width), BF16),
        in_specs=[vmem] * 3,
        out_specs=any_spec,
        scratch_shapes=[pltpu.VMEM((tokens, width), BF16), dma((tokens // 128,))],
        compiler_params=pltpu.CompilerParams(vmem_limit_bytes=16 * 1024 * 1024),
        name="norm",
    )(gated, scale, norm_gain)


def solution(mesh):
    in_specs = (
        P("ctx", "head"),
        P("ctx", "head"),
        P("ctx", None),
        P(None, "head"),
        P(),
        P("ctx", "head"),
        P("ctx", "head"),
        P("head"),
        P("head"),
        P(),
    )
    return jax.shard_map(
        functools.partial(per_device, mesh.shape["ctx"], mesh.shape["head"]),
        mesh=mesh, in_specs=in_specs, out_specs=P("ctx", "head"), check_vma=False,
    )
```

```python
import functools

import jax
import jax.numpy as jnp
from jax import lax
from jax.experimental import pallas as pl
from jax.experimental.pallas import tpu as pltpu
from jax.sharding import PartitionSpec as P

MESH = pl.DeviceIdType.MESH
F32, BF16 = jnp.float32, jnp.bfloat16
L = 128
W = 256
SECOND = 7
AHEAD = 3
UNROLL = 1
HALO = 16
KROWS = 16
NN = (((1,), (0,)), ((), ()))
NT = (((1,), (1,)), ((), ()))


def dot(a, b, dims=NN, precision=None):
    return lax.dot_general(a, b, dims, precision=precision, preferred_element_type=F32)


def iota(shape, dim):
    return lax.broadcasted_iota(jnp.int32, shape, dim)


def split2(value):
    high = value.astype(BF16)
    return high, (value - high.astype(F32)).astype(BF16)


def layer_kernel(
    n, y_count, width_all,
    docs_hbm, x_ref, z_ref, bc_ref, ld_ref, st_ref, cx_hbm, cbc_hbm, skip_hbm,
    g_ref, rx_ref,
    docs_ref, xs, zs, bcs, lds, sts, cx_ref, cbc_ref, skip_ref, xh, bch, es, m1, m2, gbm, com, cam, a_s, b_s, e_s, rows, rowsx,
    xcs, hs, yl, sz, wide, wide2, sp, ex, sc, rp, ap, ain, fw, ent, sq, sqx,
    load_sem, x_sem, z_sem, halo_send, halo_recv, ex_send, ex_recv, send1, recv1, send2, recv2,
    fw_send, fw_recv, send3, recv3,
):
    me = lax.axis_index("ctx")
    my = lax.axis_index("head")
    tokens, width = x_ref.shape
    heads = ld_ref.shape[0]
    chunks, tiles = tokens // L, width // W
    pairs = width // 128
    per_tile = W // 128
    chips = n // 2
    ppc = pairs // chips
    chip, core = me // 2, lax.rem(me, 2)
    peer = me + 1 - 2 * core
    own_rows = pl.ds(pl.multiple_of(core * 64, 64), 64)
    hd = width // heads
    first = me * tokens
    tile0 = lax.rem(chip * tiles // chips, tiles)

    def tile_at(i):
        return lax.rem(tile0 + i, tiles)

    def cols(t):
        return pl.ds(pl.multiple_of(t * W, W), W)

    def x_copy(t):
        return pltpu.make_async_copy(x_ref.at[:, cols(t)], xs.at[:, cols(t)], x_sem.at[t])

    def z_copy(t):
        return pltpu.make_async_copy(z_ref.at[:, cols(t)], zs.at[:, cols(t)], z_sem.at[t])

    barrier = pltpu.get_barrier_semaphore()

    def greet(device):
        pl.semaphore_signal(barrier, inc=1, device_id=device, device_id_type=MESH)

    greet({"ctx": peer})
    greet({"ctx": lax.rem(me + n - 1 + 2 * core, n)})
    for i in range(1, chips):
        greet({"ctx": lax.rem(me + 2 * i, n)})
    for i in range(1, y_count):
        greet({"head": lax.rem(my + i, y_count)})

    small = [
        pltpu.make_async_copy(docs_hbm, docs_ref, load_sem.at[6]),
        pltpu.make_async_copy(ld_ref, lds, load_sem.at[0]),
        pltpu.make_async_copy(st_ref, sts, load_sem.at[1]),
        pltpu.make_async_copy(bc_ref, bcs, load_sem.at[2]),
        pltpu.make_async_copy(cx_hbm, cx_ref, load_sem.at[3]),
        pltpu.make_async_copy(cbc_hbm, cbc_ref, load_sem.at[4]),
        pltpu.make_async_copy(skip_hbm, skip_ref, load_sem.at[5]),
    ]
    for copy in small:
        copy.start()
    for i in range(tiles):
        x_copy(tile_at(i)).start()

    es[...] = jnp.where(
        (iota((2 * heads, width), 1) // hd) == (iota((2 * heads, width), 0) & (heads - 1)), 1.0, 0.0
    ).astype(BF16)

    small[0].wait()
    docs = [docs_ref[i] for i in range(docs_ref.shape[0])]

    def crossed(low, high):
        hit = None
        for d in docs:
            one = (d > low) & (d <= high)
            hit = one if hit is None else hit | one
        return hit

    def put2(ref, value):
        high = value.astype(BF16).astype(F32)
        low = value - high
        for q in range(chunks):
            at = slice(q * heads, (q + 1) * heads)
            both = jnp.concatenate([high[at], low[at]], axis=0)
            ref[q * L : (q + 1) * L, :] = jnp.transpose(both).astype(BF16)

    def any_of(conditions):
        hit = conditions[0]
        for one in conditions[1:]:
            hit = hit | one
        return hit

    row8 = iota((8, 128), 0)
    for r in range(0, HALO + tokens, 8):
        starts = [d - (first - HALO + r) for d in docs]
        m1[r : r + 8, :] = jnp.where(any_of([row8 == d for d in starts]), 0.0, 1.0)
        if r >= HALO:
            both = [row8 == d for d in starts] + [row8 == d + 1 for d in starts]
            m2[r - HALO : r - HALO + 8, :] = jnp.where(any_of(both), 0.0, 1.0)
    small[1].wait()
    small[2].wait()
    small[6].wait()
    tri = jnp.where(iota((L, L), 0) <= iota((L, L), 1), 1.0, 0.0).astype(BF16)
    ld = jnp.concatenate([lds[:, q * L : (q + 1) * L] for q in range(chunks)], axis=0)
    st = jnp.concatenate([sts[:, q * L : (q + 1) * L] for q in range(chunks)], axis=0)
    high, mid = split2(ld)
    low = (ld - high.astype(F32) - mid.astype(F32)).astype(BF16)
    sums = dot(jnp.concatenate([high, mid, low], axis=0), tri)
    rows_all = chunks * heads
    lc = sums[0:rows_all] + (sums[rows_all : 2 * rows_all] + sums[2 * rows_all :])
    center, end = lc[:, L // 2 : L // 2 + 1], lc[:, L - 1 : L]
    bases = [jnp.zeros((heads, 1), F32)]
    for q in range(chunks):
        bases.append(bases[-1] + end[q * heads : (q + 1) * heads])
    base = bases[-1]
    put2(a_s, jnp.exp(lc - center))
    put2(b_s, jnp.exp(center - lc) * st)
    put2(e_s, jnp.exp(jnp.concatenate(bases[:-1], axis=0) + lc))
    centers = [center[q * heads : (q + 1) * heads] for q in range(chunks)]
    ends = [end[q * heads : (q + 1) * heads] for q in range(chunks)]

    pl.semaphore_wait(barrier, chips + 1 + y_count - 1)

    def halo_copies():
        to = {"ctx": lax.rem(me + 1, n)}
        tail = pl.ds(tokens - HALO, HALO)
        return (
            pltpu.make_async_remote_copy(
                src_ref=x_ref.at[tail, :], dst_ref=xh, send_sem=halo_send.at[0],
                recv_sem=halo_recv.at[0], device_id=to, device_id_type=MESH,
            ),
            pltpu.make_async_remote_copy(
                src_ref=bc_ref.at[tail, :], dst_ref=bch, send_sem=halo_send.at[1],
                recv_sem=halo_recv.at[1], device_id=to, device_id_type=MESH,
            ),
        )

    @pl.when(me < n - 1)
    def _():
        for copy in halo_copies():
            copy.start()

    for i in range(tiles):
        z_copy(tile_at(i)).start()

    lane = iota((heads, 128), 1)
    table = jnp.zeros((heads, 128), F32)
    for q in range(chunks):
        later = centers[q + 1] if q + 1 < chunks else jnp.zeros((heads, 1), F32)
        k = jnp.exp(ends[q] - centers[q] + later)
        b = jnp.full((heads, 1), first + q * L, jnp.int32)
        table = jnp.where(lane == q, jnp.where(crossed(b - 1, b + (L - 1)), 0.0, k), table)
        table = jnp.where(lane == chunks + q, k, table)
    b = jnp.full((heads, 1), first, jnp.int32)
    keep_all = jnp.where(crossed(b - 1, b + (tokens - 1)), 0.0, jnp.exp(base))
    table = jnp.where(lane == 2 * chunks, keep_all, table)
    rows[...] = jnp.transpose(table)[0:32, :]
    rows[2 * chunks + 1 : 2 * chunks + 2, :] = skip_ref[...]
    r_high, r_low = split2(rows[...])
    rowsx[...] = dot(r_high, es[0:heads, :]) + dot(r_low, es[0:heads, :])

    def expand_b(i, carry):
        at = pl.ds(pl.multiple_of(i * 512, 512), 512)
        xcs[:, at] = dot(b_s[...], es[:, at]).astype(BF16)
        return carry

    lax.fori_loop(0, width // 512, expand_b, 0)

    t_at = iota((L, L), 0)
    s_at = iota((L, L), 1)

    small[3].wait()
    small[4].wait()
    small[5].wait()

    def conv_half(q, block, before, taps):
        ext = jnp.concatenate([before, block], axis=0).astype(F32)
        mask1 = m1[q * L : q * L + HALO + L, :]
        mask2 = m2[q * L : (q + 1) * L, :]
        ext1 = pltpu.roll(ext, 1, 0) * jnp.concatenate([mask1, mask1], axis=1)
        near = taps[0:1, :] * ext[HALO:] + taps[1:2, :] * ext1[HALO:]
        far = taps[2:3, :] * ext[8:] + taps[3:4, :] * ext1[8:]
        far = pltpu.roll(far, 2, 0)[8:]
        return near + far * jnp.concatenate([mask2, mask2], axis=1)

    def silu_of_half(half):
        return half + half * jnp.tanh(half)

    taps_bc = cbc_ref[...].astype(F32) * 0.5

    def segment(at):
        count = 0
        for d in docs:
            count = count + jnp.where(at >= d, 1, 0)
        return count

    def shared(q, before):
        block = bcs[q * L : (q + 1) * L, :]
        both = silu_of_half(conv_half(q, block, before, taps_bc))
        b_st, c_st = both[:, :128], both[:, 128:]
        begin = first + q * L
        seg_t, seg_s = segment(t_at + begin), segment(iota((1, L), 1) + begin)
        scores = dot(c_st.astype(BF16), b_st.astype(BF16), NT)
        ok = (s_at <= t_at) & (seg_t == seg_s)
        gbm[q, 0:L, :] = jnp.where(ok, scores, 0.0).astype(BF16)
        b_kept = jnp.where(seg_t == segment(begin + L - 1), b_st, 0.0)
        gbm[q, L : 2 * L, :] = jnp.transpose(b_kept).astype(BF16)
        com[q] = jnp.where(seg_t == segment(begin - 1), c_st, 0.0).astype(BF16)
        cam[q * L : (q + 1) * L, :] = jnp.where(seg_t == segment(first - 1), c_st, 0.0).astype(BF16)

    for q in range(1, chunks):
        shared(q, bcs[q * L - HALO : q * L, :])

    @pl.when(me == 0)
    def _():
        xh[...] = jnp.zeros_like(xh)
        bch[...] = jnp.zeros_like(bch)

    @pl.when(me > 0)
    def _():
        for copy in halo_copies():
            copy.wait_recv()

    shared(0, bch[...])

    def exchange_copy(t):
        at = pl.ds(t * per_tile, per_tile)
        return pltpu.make_async_remote_copy(
            src_ref=sp.at[at, 1 - core], dst_ref=ex.at[at], send_sem=ex_send.at[t],
            recv_sem=ex_recv.at[t], device_id={"ctx": peer}, device_id_type=MESH,
        )

    def piece_copy(p):
        return pltpu.make_async_remote_copy(
            src_ref=sc.at[p], dst_ref=rp.at[chip, lax.rem(p, ppc)], send_sem=send1.at[p],
            recv_sem=recv1.at[chip * ppc + lax.rem(p, ppc)],
            device_id={"ctx": 2 * (p // ppc) + core}, device_id_type=MESH,
        )

    def keep_of(piece):
        return piece[64:65, :] + piece[65:66, :]

    def keep_rows(keep):
        high = keep.astype(BF16).astype(F32)
        row = iota((KROWS, keep.shape[1]), 0)
        return jnp.where(row == 0, high, jnp.where(row == 1, keep - high, 0.0)).astype(BF16)

    def both_cores(p):
        mine, other = sp[p, core].astype(F32), ex[p].astype(F32)
        return jnp.where(core == 0, mine, other), jnp.where(core == 0, other, mine)

    def give(t):
        exchange_copy(t).wait_recv()
        for j in range(per_tile):
            p = t * per_tile + j
            early, late = both_cores(p)
            sc[p, 0:64, :] = (keep_of(late) * early[0:64, :] + late[0:64, :]).astype(BF16)
            sc[p, 64 : 64 + KROWS, :] = keep_rows(keep_of(late) * keep_of(early))

            @pl.when(p // ppc != chip)
            def _():
                piece_copy(p).start()

            @pl.when(p // ppc == chip)
            def _():
                rp[chip, lax.rem(p, ppc)] = sc[p]

    def tile_a(t):
        x_copy(t).wait()
        taps = cx_ref[:, cols(t)].astype(F32) * 0.5
        state = jnp.zeros((128, W), F32)
        for q in range(chunks):
            at = slice(q * L, (q + 1) * L)
            block = xs[at, cols(t)]
            before = xh[:, cols(t)] if q == 0 else xs[q * L - HALO : q * L, cols(t)]
            xc = silu_of_half(conv_half(q, block, before, taps))
            xc = xc.astype(BF16)
            v = xc * xcs[at, cols(t)]
            xcs[at, cols(t)] = xc
            hs[q, :, cols(t)] = state.astype(BF16)
            both = dot(gbm[q], v)
            yl[at, cols(t)] = both[0:L, :]
            fresh = both[L:, :]
            state = (
                rowsx[q : q + 1, cols(t)] * state
                + rowsx[chunks + q : chunks + q + 1, cols(t)] * fresh
            )
        keep = rowsx[2 * chunks : 2 * chunks + 1, cols(t)]
        krows = keep_rows(keep)
        for j in range(per_tile):
            p = t * per_tile + j
            lanes = slice(j * 128, (j + 1) * 128)
            for half in range(2):
                sp[p, half, 0:64, :] = state[half * 64 : half * 64 + 64, lanes].astype(BF16)
                sp[p, half, 64 : 64 + KROWS, :] = krows[:, lanes]

    def pass_a(i, carry):
        at = [tile_at(UNROLL * i + j) for j in range(UNROLL)]
        for t in at:
            tile_a(t)
        for t in at:
            exchange_copy(t).start()

        @pl.when(i > 0)
        def _():
            for j in range(UNROLL):
                give(tile_at(UNROLL * (i - 1) + j))

        return carry

    lax.fori_loop(0, tiles // UNROLL, pass_a, 0)

    def pass_b(i, carry):
        t = tile_at(i)
        z_copy(t).wait()
        etile = es[:, cols(t)]
        skip = rowsx[2 * chunks + 1 : 2 * chunks + 2, cols(t)]
        wide[...] = dot(a_s[...], etile)
        wide2[...] = dot(e_s[...], etile)
        for q in range(chunks):
            at = slice(q * L, (q + 1) * L)
            mixed = yl[at, cols(t)] + dot(com[q], hs[q, :, cols(t)])
            own = mixed * wide[at, :] + skip * xcs[at, cols(t)].astype(F32)
            gate = silu_of_half(zs[at, cols(t)].astype(F32) * 0.5)
            yl[at, cols(t)] = own * gate
            sz[at, cols(t)] = wide2[at, :] * gate
        return carry

    lax.fori_loop(0, 1, pass_b, 0)
    for j in range(UNROLL):
        give(tile_at(tiles - UNROLL + j))
    split_b = 3
    lax.fori_loop(1, split_b, pass_b, 0)

    def piece_in(d, k):
        return pltpu.make_async_remote_copy(
            src_ref=sc.at[0], dst_ref=rp.at[d, k], send_sem=send1.at[0],
            recv_sem=recv1.at[d * ppc + k], device_id={"ctx": peer}, device_id_type=MESH,
        )

    def enter_copy(d, k):
        return pltpu.make_async_remote_copy(
            src_ref=ap.at[d, k], dst_ref=ain.at[chip * ppc + k], send_sem=send2.at[d * ppc + k],
            recv_sem=recv2.at[chip * ppc + k], device_id={"ctx": 2 * d + core}, device_id_type=MESH,
        )

    def enter_in(p):
        return pltpu.make_async_remote_copy(
            src_ref=ap.at[0, 0], dst_ref=ain.at[p], send_sem=send2.at[0],
            recv_sem=recv2.at[p], device_id={"ctx": peer}, device_id_type=MESH,
        )

    for k in range(ppc):
        for d in range(chips):
            @pl.when(d != chip)
            def _():
                piece_in(d, k).wait_recv()

        state = jnp.zeros((64, 128), F32)
        for d in range(chips):
            ap[d, k] = state.astype(BF16)
            piece = rp[d, k].astype(F32)
            state = keep_of(piece) * state + piece[0:64, :]

        def spread(i, carry):
            enter_copy(lax.rem(chip + chips - i, chips), k).start()
            return carry

        lax.fori_loop(1, chips, spread, 0)
        ain[chip * ppc + k] = ap[chip, k]


    sq[...] = jnp.zeros_like(sq)

    def forward_copy(t):
        at = pl.ds(t * per_tile, per_tile)
        return pltpu.make_async_remote_copy(
            src_ref=fw.at[at], dst_ref=ent.at[at, own_rows], send_sem=fw_send.at[t],
            recv_sem=fw_recv.at[t], device_id={"ctx": peer}, device_id_type=MESH,
        )

    def forward(t):
        for j in range(per_tile):
            p = t * per_tile + j

            @pl.when(p // ppc != chip)
            def _():
                enter_in(p).wait_recv()

            early, _ = both_cores(p)
            to_first = ain[p].astype(F32)
            to_second = keep_of(early) * to_first + early[0:64, :]
            ent[p, own_rows, :] = jnp.where(core == 0, to_first, to_second).astype(BF16)
            fw[p] = jnp.where(core == 0, to_second, to_first).astype(BF16)
        forward_copy(t).start()

    def tile_c(t):
        entering = jnp.concatenate([ent[t * per_tile + j] for j in range(per_tile)], axis=1)
        step = 2 * L
        for q in range(tokens // step):
            at = slice(q * step, (q + 1) * step)
            gated = yl[at, cols(t)] + dot(cam[at, :], entering) * sz[at, cols(t)]
            g_ref[at, cols(t)] = gated.astype(BF16)
            squares = gated * gated
            sq[at, :] += squares[:, :128] + squares[:, 128:]

    def pass_c(i, carry):
        @pl.when(i + AHEAD < tiles)
        def _():
            forward(tile_at(i + AHEAD))

        at = [tile_at(UNROLL * i + j) for j in range(UNROLL)]
        for t in at:
            forward_copy(t).wait_recv()
        for t in at:
            tile_c(t)
        return carry

    def forward_step(i, carry):
        forward(tile_at(i))
        return carry

    lax.fori_loop(split_b, SECOND, pass_b, 0)
    lax.fori_loop(0, AHEAD, forward_step, 0)
    lax.fori_loop(SECOND, tiles, pass_b, 0)
    lax.fori_loop(0, tiles // UNROLL, pass_c, 0)

    total = jnp.zeros((8, L), F32)
    for q in range(chunks):
        pick = jnp.where(iota((8, 128), 0) == q, 1.0, 0.0).astype(BF16)
        high, low = split2(sq[q * L : (q + 1) * L, :])
        total = total + dot(pick, high, NT) + dot(pick, low, NT)
    sqx[0] = total

    def sq_copy(i):
        return pltpu.make_async_remote_copy(
            src_ref=sqx.at[0], dst_ref=sqx.at[i], send_sem=send3.at[i - 1],
            recv_sem=recv3.at[i - 1], device_id={"head": lax.rem(my + i, y_count)},
            device_id_type=MESH,
        )

    for i in range(1, y_count):
        sq_copy(i).start()
    for i in range(1, y_count):
        sq_copy(i).wait_recv()
    whole = sqx[0]
    for i in range(1, y_count):
        whole = whole + sqx[i]
    scale = lax.rsqrt(whole * (1.0 / width_all) + 1e-05)
    for q in range(chunks):
        rx_ref[q * L : (q + 1) * L, :] = jnp.transpose(
            jnp.broadcast_to(scale[q : q + 1, :], (128, L))
        )

    for i in range(1, y_count):
        sq_copy(i).wait_send()

    @pl.when(me < n - 1)
    def _():
        for copy in halo_copies():
            copy.wait_send()

    for t in range(tiles):
        exchange_copy(t).wait_send()
        forward_copy(t).wait_send()

    def drain1(p, carry):
        @pl.when(p // ppc != chip)
        def _():
            piece_copy(p).wait_send()

        return carry

    lax.fori_loop(0, pairs, drain1, 0)
    for k in range(ppc):
        def drain2(i, carry):
            enter_copy(lax.rem(chip + chips - i, chips), k).wait_send()
            return carry

        lax.fori_loop(1, chips, drain2, 0)


def norm_kernel(g_ref, rx_ref, gain_ref, out_ref, stage, sem):
    rows, width = g_ref.shape
    block = 128
    gain = gain_ref[...].reshape(1, width).astype(F32)

    def copy(i):
        at = pl.ds(i * block, block)
        return pltpu.make_async_copy(stage.at[at, :], out_ref.at[at, :], sem.at[i])

    for i in range(rows // block):
        at = slice(i * block, (i + 1) * block)
        scale = rx_ref[at, :]
        for j in range(width // 128):
            lanes = slice(j * 128, (j + 1) * 128)
            stage[at, lanes] = (g_ref[at, lanes].astype(F32) * scale * gain[:, lanes]).astype(BF16)
        copy(i).start()
    for i in range(rows // block):
        copy(i).wait()


def per_device(
    n, y_count,
    x_raw, z_gate, bc_raw, conv_x, conv_bc, log_decay, step_size, skip_coef, norm_gain, doc_starts,
):
    tokens, width = x_raw.shape
    heads = log_decay.shape[1]
    chunks, tiles = tokens // L, width // W
    pairs, chips = width // 128, n // 2
    ppc = pairs // chips
    any_spec = pl.BlockSpec(memory_space=pl.ANY)
    vmem = pl.BlockSpec(memory_space=pltpu.VMEM)
    dma = pltpu.SemaphoreType.DMA
    gated, scale = pl.pallas_call(
        functools.partial(layer_kernel, n, y_count, float(width * y_count)),
        out_shape=(
            pltpu.VMEM((tokens, width), BF16),
            pltpu.VMEM((tokens, 128), F32),
        ),
        in_specs=[any_spec] * 9,
        out_specs=(vmem, vmem),
        scratch_shapes=[
            pltpu.SMEM(doc_starts.shape, jnp.int32),
            pltpu.VMEM((tokens, width), BF16),
            pltpu.VMEM((tokens, width), BF16),
            pltpu.VMEM((tokens, 256), BF16),
            pltpu.VMEM((heads, tokens), F32),
            pltpu.VMEM((heads, tokens), F32),
            pltpu.VMEM((4, width), BF16),
            pltpu.VMEM((4, 256), BF16),
            pltpu.VMEM((1, heads), F32),
            pltpu.VMEM((HALO, width), BF16),
            pltpu.VMEM((HALO, 256), BF16),
            pltpu.VMEM((2 * heads, width), BF16),
            pltpu.VMEM((HALO + tokens, 128), F32),
            pltpu.VMEM((tokens, 128), F32),
            pltpu.VMEM((chunks, 2 * L, L), BF16),
            pltpu.VMEM((chunks, L, 128), BF16),
            pltpu.VMEM((tokens, 128), BF16),
            pltpu.VMEM((tokens, 2 * heads), BF16),
            pltpu.VMEM((tokens, 2 * heads), BF16),
            pltpu.VMEM((tokens, 2 * heads), BF16),
            pltpu.VMEM((32, heads), F32),
            pltpu.VMEM((32, width), F32),
            pltpu.VMEM((tokens, width), BF16),
            pltpu.VMEM((chunks, 128, width), BF16),
            pltpu.VMEM((tokens, width), F32),
            pltpu.VMEM((tokens, width), F32),
            pltpu.VMEM((tokens, W), F32),
            pltpu.VMEM((tokens, W), F32),
            pltpu.VMEM((pairs, 2, 64 + KROWS, 128), BF16),
            pltpu.VMEM((pairs, 64 + KROWS, 128), BF16),
            pltpu.VMEM((pairs, 64 + KROWS, 128), BF16),
            pltpu.VMEM((chips, ppc, 64 + KROWS, 128), BF16),
            pltpu.VMEM((chips, ppc, 64, 128), BF16),
            pltpu.VMEM((pairs, 64, 128), BF16),
            pltpu.VMEM((pairs, 64, 128), BF16),
            pltpu.VMEM((pairs, 128, 128), BF16),
            pltpu.VMEM((tokens, 128), F32),
            pltpu.VMEM((y_count, 8, 128), F32),
            dma((7,)), dma((tiles,)), dma((tiles,)), dma((2,)), dma((2,)),
            dma((tiles,)), dma((tiles,)), dma((pairs,)), dma((pairs,)), dma((pairs,)), dma((pairs,)),
            dma((tiles,)), dma((tiles,)),
            dma((y_count,)), dma((y_count,)),
        ],
        compiler_params=pltpu.CompilerParams(
            collective_id=0, has_side_effects=True, vmem_limit_bytes=59 * 1024 * 1024
        ),
        name="layer",
    )(
        doc_starts, x_raw, z_gate, bc_raw, log_decay.T, step_size.T, conv_x, conv_bc,
        skip_coef.reshape(1, heads),
    )
    return pl.pallas_call(
        norm_kernel,
        out_shape=jax.ShapeDtypeStruct((tokens, width), BF16),
        in_specs=[vmem] * 3,
        out_specs=any_spec,
        scratch_shapes=[pltpu.VMEM((tokens, width), BF16), dma((tokens // 128,))],
        compiler_params=pltpu.CompilerParams(vmem_limit_bytes=16 * 1024 * 1024),
        name="norm",
    )(gated, scale, norm_gain)


def solution(mesh):
    in_specs = (
        P("ctx", "head"),
        P("ctx", "head"),
        P("ctx", None),
        P(None, "head"),
        P(),
        P("ctx", "head"),
        P("ctx", "head"),
        P("head"),
        P("head"),
        P(),
    )
    return jax.shard_map(
        functools.partial(per_device, mesh.shape["ctx"], mesh.shape["head"]),
        mesh=mesh, in_specs=in_specs, out_specs=P("ctx", "head"), check_vma=False,
    )
```
